32 devices in a mesh: groups: 2 (over y), seq: 4 (over z), heads: 2 (over x), sub: 2 (over core).
Axes of the slice: x: 2, y: 2, z: 4, core: 2. Of those that a mesh axis runs over, the one named last changes fastest.
Arguments:
- queries: bfloat16 [8192, 1024], P(('groups', 'seq', 'heads'), 'sub'), parts along dimension 0, may hold values from -6 to 6
- keys: bfloat16 [8192, 1024], P(('groups', 'seq', 'heads'), 'sub'), parts along dimension 0, may hold values from -6 to 6
- values: bfloat16 [8192, 1024], P(('groups', 'seq', 'heads'), 'sub'), parts along dimension 0, may hold values from -6 to 6
- out_grad: bfloat16 [8192, 1024], P(('groups', 'seq', 'heads'), 'sub'), parts along dimension 0, may hold values from -6 to 6
- level_weights: float32 [8, 8, 8192], P('sub', None, ('groups', 'seq', 'heads')), parts along dimension 2, may hold values from 0.25 to 2
Outputs:
- grad_queries: bfloat16 [8192, 1024], P(('groups', 'seq', 'heads'), 'sub'), parts along dimension 0
- grad_keys: bfloat16 [8192, 1024], P(('groups', 'seq', 'heads'), 'sub'), parts along dimension 0
- grad_values: bfloat16 [8192, 1024], P(('groups', 'seq', 'heads'), 'sub'), parts along dimension 0
- weight_grads: float32 [8, 8, 8192], P('sub', None, ('groups', 'seq', 'heads')), parts along dimension 2
The draws below stay inside these ranges and needn't reach their ends.
There are 2 independent parts, one for each index of `groups`. The reference program is written for one: setup_inputs(seed, part) draws one part's arguments, and reference() takes and returns one part's arrays. A program takes and returns all parts, laid end to end along the dimension named above; each array names one. Nothing has to cross between parts.
All inputs are finite; a program needn't handle non-finite values.
Results may differ from the reference program's by a relative error of at most 0.0056.
Values may be sent and summed in bfloat16 or wider, within the bound.
No kernel may reach another device: no remote copies, remote signals or barrier semaphores. Data moves between devices by JAX's collectives and lax.ppermute only.
A program may use at most 64 MiB of HBM per device.

```python
import math
import jax
import jax.numpy as jnp
from jax import lax

DH = 128
HEADS = 8
LEVELS = 8
TOK_DEV = 512
TOKENS = 4096


def level_of(own_key, extent, pieces, low, top_value):
    def one(position, parts):
        draws = jax.random.uniform(jax.random.fold_in(jax.random.fold_in(own_key, 6), position), (parts,), jnp.float32, low / len(pieces), top_value / len(pieces))
        return jnp.repeat(jnp.exp(draws), extent[position] // parts).reshape((-1,) + (1,) * (len(extent) - position - 1))

    level = one(*pieces[0])
    for cut in pieces[1:]:
        level = level * one(*cut)
    return level


def centred(own_key, shape, scale, most, shards=(), held_as=jnp.bfloat16):
    loudness = level_of(own_key, shape, shards, -0.22, 0.18) if shards else 1.0
    result = jax.random.normal(own_key, shape, jnp.float32) * scale * loudness
    return jnp.minimum(jnp.maximum(result, -most), most).astype(held_as)


def setup_inputs(seed: int = 0, part: int = 0) -> dict:
    seeds = jax.random.split(jax.random.key(seed), 6)
    part_keys = jax.random.split(jax.random.fold_in(seeds[5], part), 6)
    return {
        "queries": centred(part_keys[0], (TOKENS, HEADS * DH), 1.0, 6.0, ((0, 8), (1, 2))),
        "keys": centred(part_keys[1], (TOKENS, HEADS * DH), 1.0, 6.0, ((0, 8), (1, 2))),
        "values": centred(part_keys[2], (TOKENS, HEADS * DH), 1.0, 6.0, ((0, 8), (1, 2))),
        "out_grad": centred(part_keys[3], (TOKENS, HEADS * DH), 1.0, 6.0, ((0, 8), (1, 2))),
        "level_weights": jnp.clip(jnp.exp(math.log(2.0) - 2.0794415 * jax.random.uniform(part_keys[4], (HEADS, LEVELS, TOKENS), jnp.float32) ** level_of(part_keys[4], (HEADS, LEVELS, TOKENS), ((0, 2), (2, 8)), -0.2, 0.2)), 0.25, 2.0),
    }


def to_low(array_in):
    return lax.optimization_barrier(array_in.astype(jnp.bfloat16)).astype(jnp.float32)

def inner_block(queries_c, keys_c, values_c, grads_c, gate_zero, scale_zero):
    query_f = queries_c.astype(jnp.float32)
    key_f = keys_c.astype(jnp.float32)
    value_f = values_c.astype(jnp.float32)
    grad_f = grads_c.astype(jnp.float32)
    tok_rows = queries_c.shape[0]
    causal = jnp.tril(jnp.ones((tok_rows, tok_rows), dtype=bool))
    scores = jnp.einsum('thd,shd->hts', query_f, key_f)
    grad_dots = jnp.einsum('thd,shd->hts', grad_f, value_f)
    scores = jnp.where(causal, scores, jnp.float32(0.0))
    grad_dots = jnp.where(causal, grad_dots, jnp.float32(0.0))
    near_weight = scale_zero * lax.optimization_barrier(jnp.sum(scores * grad_dots, axis=2))
    factor = scale_zero * gate_zero[:, :, None]
    grad_mix = to_low(factor * grad_dots)
    score_mix = to_low(factor * scores)
    near_q = jnp.einsum('hts,shd->thd', grad_mix, key_f)
    near_k = jnp.einsum('hts,thd->shd', grad_mix, query_f)
    near_v = jnp.einsum('hts,thd->shd', score_mix, grad_f)
    return (near_q, near_k, near_v, near_weight)

def reference(queries, keys, values, out_grad, level_weights):
    tok_rows = TOK_DEV
    blocks_n = TOKENS // tok_rows
    head_count = HEADS
    head_width = DH
    shape_four = (blocks_n, tok_rows, head_count, head_width)
    query_h = queries.reshape(shape_four)
    key_h = keys.reshape(shape_four)
    value_h = values.reshape(shape_four)
    grad_h = out_grad.reshape(shape_four)
    gates = level_weights.astype(jnp.float32).reshape(head_count, LEVELS, blocks_n, tok_rows)
    bit_count = blocks_n.bit_length() - 1
    base_scale = 1.0 / math.sqrt(head_width * tok_rows)
    scales = [base_scale] + [base_scale / math.sqrt(2.0 ** (level_idx - 1)) for level_idx in range(1, LEVELS)]
    gate_zero = jnp.transpose(gates[:, 0], (1, 0, 2))

    def one_block(items):
        return inner_block(items[0], items[1], items[2], items[3], items[4], scales[0])
    near_q, near_k, near_v, near_weight = lax.map(one_block, (query_h, key_h, value_h, grad_h, gate_zero))
    query_f = query_h.astype(jnp.float32)
    key_f = key_h.astype(jnp.float32)
    value_f = value_h.astype(jnp.float32)
    grad_f = grad_h.astype(jnp.float32)
    key_state = jnp.einsum('cshd,cshe->chde', key_f, value_f)
    reverse_sum = jnp.zeros_like(key_state)
    grad_q = near_q
    weight_rows = [near_weight]
    for level_idx in range(1, LEVELS):
        if level_idx > bit_count:
            weight_rows.append(jnp.zeros_like(near_weight))
            continue
        half = 2 ** (level_idx - 1)
        group_n = blocks_n // (2 * half)
        split_shape = (group_n, 2, half, head_count, head_width, head_width)
        split = key_state.reshape(split_shape)
        lower = lax.optimization_barrier(jnp.sum(split[:, 0], axis=1))
        sibling = jnp.stack([jnp.zeros_like(lower), lower], axis=1)[:, :, None]
        sibling = jnp.broadcast_to(sibling, split_shape).reshape(key_state.shape)
        state_low = to_low(sibling)
        products = jnp.einsum('cthe,chde->cthd', grad_f, state_low)
        gate_now = jnp.transpose(gates[:, level_idx], (1, 2, 0))
        grad_q = grad_q + scales[level_idx] * gate_now[..., None] * products
        weight_rows.append(jnp.transpose(scales[level_idx] * lax.optimization_barrier(jnp.sum(products * query_f, axis=3)), (0, 2, 1)))
        scaled = to_low(gate_now[..., None] * query_f)
        grad_state = scales[level_idx] * jnp.einsum('cthd,cthe->chde', scaled, grad_f)
        split_grad = grad_state.reshape(split_shape)
        upper = lax.optimization_barrier(jnp.sum(split_grad[:, 1], axis=1))
        toward = jnp.stack([upper, jnp.zeros_like(upper)], axis=1)[:, :, None]
        toward = jnp.broadcast_to(toward, split_shape).reshape(key_state.shape)
        reverse_sum = reverse_sum + toward
    reverse_low = to_low(reverse_sum)
    grad_k = near_k + jnp.einsum('cshe,chde->cshd', value_f, reverse_low)
    grad_v = near_v + jnp.einsum('cshd,chde->cshe', key_f, reverse_low)
    flat = (TOKENS, head_count * head_width)
    stacked = jnp.stack(weight_rows, axis=0)
    weight_grads = jnp.transpose(stacked, (2, 0, 1, 3)).reshape(head_count, LEVELS, TOKENS)
    return (grad_q.reshape(flat).astype(jnp.bfloat16), grad_k.reshape(flat).astype(jnp.bfloat16), grad_v.reshape(flat).astype(jnp.bfloat16), weight_grads)
```

```python
import functools
import math

import jax
import jax.numpy as jnp
from jax import lax
from jax.experimental import pallas as pl
from jax.experimental.pallas import tpu as pltpu
from jax.sharding import PartitionSpec as P

AXES = ("seq", "heads")
LOW = jnp.bfloat16
ROWS = 256


def nt(left, right):
    return lax.dot_general(
        left, right, (((1,), (1,)), ((), ())), preferred_element_type=jnp.float32
    )


def nn(left, right):
    return jnp.dot(left, right, preferred_element_type=jnp.float32)


def flip(block, mask):
    size = lax.axis_size(AXES)
    return lax.ppermute(block, AXES, [(i, i ^ mask) for i in range(size)])


def block_index():
    return lax.axis_index("seq") * lax.axis_size("heads") + lax.axis_index("heads")


def in_vmem(array):
    return pltpu.with_memory_space_constraint(array, pltpu.VMEM)


def level_scales(width, tokens, count):
    base = 1.0 / math.sqrt(width * tokens)
    return [base] + [base / math.sqrt(2.0 ** (level - 1)) for level in range(1, count)]


def state_kernel(
    bits, scales, q_hbm, k_hbm, v_hbm, g_hbm, w_hbm,
    q_out, k_out, v_out, g_out, w_out, qt_out, kt_out, d1_out, own_out, other_out, far_out, sems, w_sem,
):
    heads, tokens, width = q_out.shape
    half = heads // 2
    pairs = ((q_hbm, q_out), (k_hbm, k_out), (v_hbm, v_out), (g_hbm, g_out))
    w_copy = pltpu.make_async_copy(w_hbm, w_out, w_sem)
    copies = [
        [
            pltpu.make_async_copy(src.at[:, pl.ds(h * width, width)], dst.at[h], sems.at[i, h])
            for i, (src, dst) in enumerate(pairs)
        ]
        for h in range(heads)
    ]
    w_copy.start()
    for group in copies:
        for copy in group:
            copy.start()
    place = block_index()
    low_bit = place & 1
    w_copy.wait()
    for h in range(heads):
        for copy in copies[h]:
            copy.wait()
        query_t = q_out[h].T
        key_t = k_out[h].T
        qt_out[h] = query_t
        kt_out[h] = key_t
        grad = g_out[h]
        state = nn(key_t, v_out[h])
        query_f = query_t.astype(jnp.float32)
        slot = (h // half) ^ low_bit
        for level in range(1, bits + 1):
            scaled = (w_out[h, pl.ds(level, 1), :] * query_f).astype(LOW)
            level_state = scales[level] * nn(scaled, grad)
            upper = ((place >> (level - 1)) & 1) == 1
            mixed = jnp.where(upper, level_state, state).astype(LOW)
            if level == 1:
                d1_out[h] = mixed
            else:
                row = (level - 2) * half + h % half

                @pl.when(slot == 0)
                def _():
                    own_out[row] = mixed

                @pl.when(slot == 1)
                def _():
                    other_out[row] = mixed
                    if level > 2:
                        far_out[row - half] = mixed


def near_kernel(
    first, scale, q_ref, k_ref, v_ref, g_ref, w_ref, kt_ref, nq_out, nk_out, nv_out, nw_out
):
    heads, width, tokens = nq_out.shape
    rows = min(ROWS, tokens)
    for local in range(heads):
        h = first + local
        factor = scale * w_ref[h, pl.ds(0, 1), :]
        total = None
        weight = None
        for start in range(0, tokens, rows):
            left = tokens - start
            key = k_ref[h, start : start + rows, :]
            value = v_ref[h, start : start + rows, :]
            query = q_ref[h, start:, :]
            grad = g_ref[h, start:, :]
            scores = nt(key, query)
            dots = nt(value, grad)
            allowed = lax.broadcasted_iota(jnp.int32, (rows, left), 0) <= lax.broadcasted_iota(
                jnp.int32, (rows, left), 1
            )
            scores = jnp.where(allowed, scores, 0.0)
            dots = jnp.where(allowed, dots, 0.0)
            part = jnp.sum(scores * dots, axis=0, keepdims=True)
            now = factor[:, start:]
            grad_mix = (now * dots).astype(LOW)
            score_mix = (now * scores).astype(LOW)
            nk_out[local, start : start + rows, :] = nn(grad_mix, query)
            nv_out[local, start : start + rows, :] = nn(score_mix, grad)
            back = nn(kt_ref[h, :, start : start + rows], grad_mix)
            if start == 0:
                nq_out[local] = back
                nw_out[local] = scale * part
            else:
                nq_out[local, :, start:] += back
                nw_out[local, :, start:] += scale * part


def far_kernel(bits, scales, split, *refs):
    (k_ref, v_ref, g_ref, w_ref, qt_ref, r1_ref, own_ref, other_ref), refs = refs[:8], refs[8:]
    near = [refs[4 * i : 4 * i + 4] for i in range(len(split))]
    gq_hbm, gk_hbm, gv_hbm, gw_out, gq_buf, gk_buf, gv_buf, sems = refs[4 * len(split) :]
    heads, tokens, width = k_ref.shape
    half = heads // 2
    place = block_index()
    low_bit = place & 1
    copies = []
    for h in range(heads):
        index = max(i for i, first in enumerate(split) if first <= h)
        nq_ref, nk_ref, nv_ref, nw_ref = near[index]
        local = h - split[index]
        grad = g_ref[h]
        query_t = qt_ref[h].astype(jnp.float32)
        reverse = jnp.zeros((width, width), jnp.float32)
        total = nq_ref[local]
        gw_out[h] = jnp.zeros(gw_out.shape[1:], jnp.float32)
        gw_out[h, pl.ds(0, 1), :] = nw_ref[local]
        for level in range(1, bits + 1):
            if level == 1:
                got = r1_ref[h]
            else:
                row = (level - 2) * half + h % half
                got = jnp.where(low_bit == h // half, own_ref[row], other_ref[row])
            upper = ((place >> (level - 1)) & 1) == 1
            got_f = got.astype(jnp.float32)
            sibling = jnp.where(upper, got_f, 0.0).astype(LOW)
            reverse = reverse + jnp.where(upper, 0.0, got_f)
            products = scales[level] * nt(sibling, grad)
            total = total + w_ref[h, pl.ds(level, 1), :] * products
            gw_out[h, pl.ds(level, 1), :] = jnp.sum(products * query_t, axis=0, keepdims=True)
        low = reverse.astype(LOW)
        gq_buf[h] = total.T.astype(LOW)
        gk_buf[h] = (nk_ref[local] + nt(v_ref[h], low)).astype(LOW)
        gv_buf[h] = (nv_ref[local] + nn(k_ref[h], low)).astype(LOW)
        for i, (buf, hbm) in enumerate(((gq_buf, gq_hbm), (gk_buf, gk_hbm), (gv_buf, gv_hbm))):
            copy = pltpu.make_async_copy(buf.at[h], hbm.at[:, pl.ds(h * width, width)], sems.at[i, h])
            copy.start()
            copies.append(copy)
    for copy in copies:
        copy.wait()


ANY = pl.BlockSpec(memory_space=pl.ANY)
IN_VMEM = pl.BlockSpec(memory_space=pltpu.VMEM)
LIMIT = 48 * 1024 * 1024


def on_device(queries, keys, values, out_grad, level_weights):
    tokens = queries.shape[0]
    heads, levels, _ = level_weights.shape
    width = queries.shape[1] // heads
    half = heads // 2
    bits = lax.axis_size(AXES).bit_length() - 1
    scales = level_scales(width, tokens, levels)
    by_head = pltpu.VMEM((heads, tokens, width), LOW)
    by_head_t = pltpu.VMEM((heads, width, tokens), LOW)
    halves = (bits - 1) * half
    (q_v, k_v, v_v, g_v, w_v, qt, kt, d1, own, other, far) = pl.pallas_call(
        functools.partial(state_kernel, bits, scales),
        out_shape=(
            by_head, by_head, by_head, by_head,
            pltpu.VMEM((heads, levels, tokens), jnp.float32),
            by_head_t, by_head_t,
            pltpu.VMEM((heads, width, width), LOW),
            pltpu.VMEM((halves, width, width), LOW),
            pltpu.VMEM((halves, width, width), LOW),
            pltpu.VMEM((halves - half, width, width), LOW),
        ),
        in_specs=[ANY] * 5,
        out_specs=(IN_VMEM,) * 11,
        scratch_shapes=[pltpu.SemaphoreType.DMA((4, heads)), pltpu.SemaphoreType.DMA],
        compiler_params=pltpu.CompilerParams(vmem_limit_bytes=LIMIT),
        cost_estimate=pl.CostEstimate(
            flops=2 * heads * (bits + 1) * tokens * width * width,
            bytes_accessed=4 * heads * tokens * width * 2,
            transcendentals=0,
        ),
        name="states",
    )(queries, keys, values, out_grad, level_weights)

    def near(first, count):
        return pl.pallas_call(
            functools.partial(near_kernel, first, scales[0]),
            out_shape=(
                pltpu.VMEM((count, width, tokens), jnp.float32),
                pltpu.VMEM((count, tokens, width), jnp.float32),
                pltpu.VMEM((count, tokens, width), jnp.float32),
                pltpu.VMEM((count, 1, tokens), jnp.float32),
            ),
            in_specs=[IN_VMEM] * 6,
            out_specs=(IN_VMEM,) * 4,
            compiler_params=pltpu.CompilerParams(vmem_limit_bytes=LIMIT),
            cost_estimate=pl.CostEstimate(
                flops=10 * count * tokens * tokens * width,
                bytes_accessed=count * tokens * width * 20,
                transcendentals=0,
            ),
            name="near",
        )(*[in_vmem(x) for x in (q_v, k_v, v_v, g_v, w_v, kt)])

    split = (0, half)
    near_parts = [near(0, half), near(half, heads - half)]

    got_x = flip(other, 1)
    got_1 = flip(d1, 1)
    got_z = flip(own[half:], 2)
    got_d = flip(far, 3)
    as_f = lambda x: x.astype(jnp.float32)
    pair = (as_f(own[:half]) + as_f(got_x[:half])).astype(LOW)
    quad = as_f(own[half:]) + as_f(got_x[half:]) + as_f(got_z) + as_f(got_d)
    sums = [pair]
    for bit in range(2, bits):
        sums.append(quad[:half].astype(LOW))
        quad = quad[half:]
        if bit < bits - 1:
            quad = quad + as_f(flip(quad.astype(LOW), 1 << bit))
    own_half = [flip(x, 1 << (i + 1)) for i, x in enumerate(sums)]
    other_half = [flip(x, (1 << (i + 1)) ^ 1) for i, x in enumerate(sums)]
    out = jax.ShapeDtypeStruct((tokens, heads * width), LOW)
    flat_near = [x for part in near_parts for x in part]
    return pl.pallas_call(
        functools.partial(far_kernel, bits, scales, split),
        out_shape=(out, out, out, jax.ShapeDtypeStruct((heads, levels, tokens), jnp.float32)),
        in_specs=[IN_VMEM] * (8 + len(flat_near)),
        out_specs=(ANY, ANY, ANY, IN_VMEM),
        scratch_shapes=[pltpu.VMEM((heads, tokens, width), LOW)] * 3
        + [pltpu.SemaphoreType.DMA((3, heads))],
        compiler_params=pltpu.CompilerParams(vmem_limit_bytes=LIMIT),
        cost_estimate=pl.CostEstimate(
            flops=2 * heads * (bits + 2) * tokens * width * width,
            bytes_accessed=3 * heads * tokens * width * 2,
            transcendentals=0,
        ),
        name="far",
    )(
        *[
            in_vmem(x)
            for x in (
                k_v, v_v, g_v, w_v, qt, got_1,
                jnp.concatenate(own_half, 0), jnp.concatenate(other_half, 0), *flat_near,
            )
        ]
    )


def solution(mesh):
    rows = P(("groups", "seq", "heads"), "sub")
    weights = P("sub", None, ("groups", "seq", "heads"))
    return jax.shard_map(
        on_device,
        mesh=mesh,
        in_specs=(rows, rows, rows, rows, weights),
        out_specs=(rows, rows, rows, weights),
        check_vma=False,
    )
```

```python
import functools
import math

import jax
import jax.numpy as jnp
from jax import lax
from jax.experimental import pallas as pl
from jax.experimental.pallas import tpu as pltpu
from jax.sharding import PartitionSpec as P

AXES = ("seq", "heads")
LOW = jnp.bfloat16
ROWS = 256


def nt(left, right):
    return lax.dot_general(
        left, right, (((1,), (1,)), ((), ())), preferred_element_type=jnp.float32
    )


def nn(left, right):
    return jnp.dot(left, right, preferred_element_type=jnp.float32)


def flip(block, mask):
    size = lax.axis_size(AXES)
    return lax.ppermute(block, AXES, [(i, i ^ mask) for i in range(size)])


def block_index():
    return lax.axis_index("seq") * lax.axis_size("heads") + lax.axis_index("heads")


def in_vmem(array):
    return pltpu.with_memory_space_constraint(array, pltpu.VMEM)


def level_scales(width, tokens, count):
    base = 1.0 / math.sqrt(width * tokens)
    return [base] + [base / math.sqrt(2.0 ** (level - 1)) for level in range(1, count)]


def state_kernel(
    bits, scales, q_hbm, k_hbm, v_hbm, g_hbm, w_hbm,
    q_out, k_out, v_out, g_out, w_out, qt_out, kt_out, d1_out, own_out, other_out, far_out, sems, w_sem,
):
    heads, tokens, width = q_out.shape
    half = heads // 2
    pairs = ((q_hbm, q_out), (k_hbm, k_out), (v_hbm, v_out), (g_hbm, g_out))
    w_copy = pltpu.make_async_copy(w_hbm, w_out, w_sem)
    copies = [
        [
            pltpu.make_async_copy(src.at[:, pl.ds(h * width, width)], dst.at[h], sems.at[i, h])
            for i, (src, dst) in enumerate(pairs)
        ]
        for h in range(heads)
    ]
    w_copy.start()
    for group in copies:
        for copy in group:
            copy.start()
    place = block_index()
    low_bit = place & 1
    w_copy.wait()
    for h in range(heads):
        for copy in copies[h]:
            copy.wait()
        query_t = q_out[h].T
        key_t = k_out[h].T
        qt_out[h] = query_t
        kt_out[h] = key_t
        grad = g_out[h]
        state = nn(key_t, v_out[h])
        query_f = query_t.astype(jnp.float32)
        slot = (h // half) ^ low_bit
        for level in range(1, bits + 1):
            scaled = (w_out[h, pl.ds(level, 1), :] * query_f).astype(LOW)
            level_state = scales[level] * nn(scaled, grad)
            upper = ((place >> (level - 1)) & 1) == 1
            mixed = jnp.where(upper, level_state, state).astype(LOW)
            if level == 1:
                d1_out[h] = mixed
            else:
                row = (level - 2) * half + h % half

                @pl.when(slot == 0)
                def _():
                    own_out[row] = mixed

                @pl.when(slot == 1)
                def _():
                    other_out[row] = mixed
                    if level > 2:
                        far_out[row - half] = mixed


def near_kernel(
    first, scale, q_ref, k_ref, v_ref, g_ref, w_ref, kt_ref, *refs
):
    if first == 0:
        refs[-1][...] = refs[0][...]
        refs = refs[1:-1]
    nq_out, nk_out, nv_out, nw_out = refs
    heads, width, tokens = nq_out.shape
    rows = min(ROWS, tokens)
    for local in range(heads):
        h = first + local
        factor = scale * w_ref[h, pl.ds(0, 1), :]
        total = None
        weight = None
        for start in range(0, tokens, rows):
            left = tokens - start
            key = k_ref[h, start : start + rows, :]
            value = v_ref[h, start : start + rows, :]
            query = q_ref[h, start:, :]
            grad = g_ref[h, start:, :]
            scores = nt(key, query)
            dots = nt(value, grad)
            allowed = lax.broadcasted_iota(jnp.int32, (rows, left), 0) <= lax.broadcasted_iota(
                jnp.int32, (rows, left), 1
            )
            scores = jnp.where(allowed, scores, 0.0)
            dots = jnp.where(allowed, dots, 0.0)
            part = jnp.sum(scores * dots, axis=0, keepdims=True)
            now = factor[:, start:]
            grad_mix = (now * dots).astype(LOW)
            score_mix = (now * scores).astype(LOW)
            nk_out[local, start : start + rows, :] = nn(grad_mix, query)
            nv_out[local, start : start + rows, :] = nn(score_mix, grad)
            back = nn(kt_ref[h, :, start : start + rows], grad_mix)
            if start == 0:
                nq_out[local] = back
                nw_out[local] = scale * part
            else:
                nq_out[local, :, start:] += back
                nw_out[local, :, start:] += scale * part


def far_kernel(bits, scales, split, *refs):
    (k_ref, v_ref, g_ref, w_ref, qt_ref, r1_ref), refs = refs[:6], refs[6:]
    own_refs, other_refs, refs = refs[: bits - 1], refs[bits - 1 : 2 * bits - 2], refs[2 * bits - 2 :]
    near = [refs[4 * i : 4 * i + 4] for i in range(len(split))]
    gq_hbm, gk_hbm, gv_hbm, gw_out, gq_buf, gk_buf, gv_buf, sems = refs[4 * len(split) :]
    heads, tokens, width = k_ref.shape
    half = heads // 2
    place = block_index()
    low_bit = place & 1
    copies = []
    for h in range(heads):
        index = max(i for i, first in enumerate(split) if first <= h)
        nq_ref, nk_ref, nv_ref, nw_ref = near[index]
        local = h - split[index]
        grad = g_ref[h]
        query_t = qt_ref[h].astype(jnp.float32)
        reverse = jnp.zeros((width, width), jnp.float32)
        total = nq_ref[local]
        gw_out[h] = jnp.zeros(gw_out.shape[1:], jnp.float32)
        gw_out[h, pl.ds(0, 1), :] = nw_ref[local]
        for level in range(1, bits + 1):
            if level == 1:
                got = r1_ref[h]
            else:
                own_ref, other_ref = own_refs[level - 2], other_refs[level - 2]
                got = jnp.where(low_bit == h // half, own_ref[h % half], other_ref[h % half])
            upper = ((place >> (level - 1)) & 1) == 1
            got_f = got.astype(jnp.float32)
            sibling = jnp.where(upper, got_f, 0.0).astype(LOW)
            reverse = reverse + jnp.where(upper, 0.0, got_f)
            products = scales[level] * nt(sibling, grad)
            total = total + w_ref[h, pl.ds(level, 1), :] * products
            gw_out[h, pl.ds(level, 1), :] = jnp.sum(products * query_t, axis=0, keepdims=True)
        low = reverse.astype(LOW)
        gq_buf[h] = total.T.astype(LOW)
        gk_buf[h] = (nk_ref[local] + nt(v_ref[h], low)).astype(LOW)
        gv_buf[h] = (nv_ref[local] + nn(k_ref[h], low)).astype(LOW)
        for i, (buf, hbm) in enumerate(((gq_buf, gq_hbm), (gk_buf, gk_hbm), (gv_buf, gv_hbm))):
            copy = pltpu.make_async_copy(buf.at[h], hbm.at[:, pl.ds(h * width, width)], sems.at[i, h])
            copy.start()
            copies.append(copy)
    for copy in copies:
        copy.wait()


ANY = pl.BlockSpec(memory_space=pl.ANY)
IN_VMEM = pl.BlockSpec(memory_space=pltpu.VMEM)
LIMIT = 48 * 1024 * 1024


def on_device(queries, keys, values, out_grad, level_weights):
    tokens = queries.shape[0]
    heads, levels, _ = level_weights.shape
    width = queries.shape[1] // heads
    half = heads // 2
    bits = lax.axis_size(AXES).bit_length() - 1
    scales = level_scales(width, tokens, levels)
    by_head = pltpu.VMEM((heads, tokens, width), LOW)
    by_head_t = pltpu.VMEM((heads, width, tokens), LOW)
    halves = (bits - 1) * half
    (q_v, k_v, v_v, g_v, w_v, qt, kt, d1, own, other, far) = pl.pallas_call(
        functools.partial(state_kernel, bits, scales),
        out_shape=(
            by_head, by_head, by_head, by_head,
            pltpu.VMEM((heads, levels, tokens), jnp.float32),
            by_head_t, by_head_t,
            pltpu.VMEM((heads, width, width), LOW),
            pltpu.VMEM((halves, width, width), LOW),
            pltpu.VMEM((halves, width, width), LOW),
            pltpu.VMEM((halves - half, width, width), LOW),
        ),
        in_specs=[ANY] * 5,
        out_specs=(IN_VMEM,) * 11,
        scratch_shapes=[pltpu.SemaphoreType.DMA((4, heads)), pltpu.SemaphoreType.DMA],
        compiler_params=pltpu.CompilerParams(vmem_limit_bytes=LIMIT),
        cost_estimate=pl.CostEstimate(
            flops=2 * heads * (bits + 1) * tokens * width * width,
            bytes_accessed=4 * heads * tokens * width * 2,
            transcendentals=0,
        ),
        name="states",
    )(*[pltpu.with_memory_space_constraint(x, pltpu.HBM) for x in (queries, keys, values, out_grad, level_weights)])

    def near(first, count, passed=()):
        return pl.pallas_call(
            functools.partial(near_kernel, first, scales[0]),
            out_shape=(
                pltpu.VMEM((count, width, tokens), jnp.float32),
                pltpu.VMEM((count, tokens, width), jnp.float32),
                pltpu.VMEM((count, tokens, width), jnp.float32),
                pltpu.VMEM((count, 1, tokens), jnp.float32),
                *[pltpu.VMEM(x.shape, x.dtype) for x in passed],
            ),
            in_specs=[IN_VMEM] * (6 + len(passed)),
            out_specs=(IN_VMEM,) * (4 + len(passed)),
            compiler_params=pltpu.CompilerParams(vmem_limit_bytes=LIMIT),
            cost_estimate=pl.CostEstimate(
                flops=1000 * count * tokens * tokens * width,
                bytes_accessed=count * tokens * width * 20,
                transcendentals=0,
            ),
            name="near",
        )(*[in_vmem(x) for x in (q_v, k_v, v_v, g_v, w_v, kt, *passed)])

    split = (0, half)
    near_parts = [near(0, half, (d1,)), near(half, heads - half)]
    d1 = near_parts[0][-1]

    got_x = flip(other, 1)
    got_1 = flip(d1, 1)
    got_z = flip(own[half:], 2)
    got_d = flip(far, 3)
    as_f = lambda x: x.astype(jnp.float32)
    pair = (as_f(own[:half]) + as_f(got_x[:half])).astype(LOW)
    quad = as_f(own[half:]) + as_f(got_x[half:]) + as_f(got_z) + as_f(got_d)
    sums = [pair]
    for bit in range(2, bits):
        sums.append(quad[:half].astype(LOW))
        quad = quad[half:]
        if bit < bits - 1:
            quad = quad + as_f(flip(quad.astype(LOW), 1 << bit))
    own_half = [flip(x, 1 << (i + 1)) for i, x in enumerate(sums)]
    other_half = [flip(x, (1 << (i + 1)) ^ 1) for i, x in enumerate(sums)]
    out = jax.ShapeDtypeStruct((tokens, heads * width), LOW)
    operands = [k_v, v_v, g_v, w_v, qt, got_1, *own_half, *other_half]
    operands += [x for part in near_parts for x in part[:4]]
    return pl.pallas_call(
        functools.partial(far_kernel, bits, scales, split),
        out_shape=(out, out, out, jax.ShapeDtypeStruct((heads, levels, tokens), jnp.float32)),
        in_specs=[IN_VMEM] * len(operands),
        out_specs=(ANY, ANY, ANY, IN_VMEM),
        scratch_shapes=[pltpu.VMEM((heads, tokens, width), LOW)] * 3
        + [pltpu.SemaphoreType.DMA((3, heads))],
        compiler_params=pltpu.CompilerParams(vmem_limit_bytes=LIMIT),
        cost_estimate=pl.CostEstimate(
            flops=2 * heads * (bits + 2) * tokens * width * width,
            bytes_accessed=3 * heads * tokens * width * 2,
            transcendentals=0,
        ),
        name="far",
    )(*[in_vmem(x) for x in operands])


def solution(mesh):
    rows = P(("groups", "seq", "heads"), "sub")
    weights = P("sub", None, ("groups", "seq", "heads"))
    return jax.shard_map(
        on_device,
        mesh=mesh,
        in_specs=(rows, rows, rows, rows, weights),
        out_specs=(rows, rows, rows, weights),
        check_vma=False,
    )
```

```python
import functools
import math

import jax
import jax.numpy as jnp
from jax import lax
from jax.experimental import pallas as pl
from jax.experimental.pallas import tpu as pltpu
from jax.sharding import PartitionSpec as P

AXES = ("seq", "heads")
LOW = jnp.bfloat16
ROWS = 256


def nt(left, right):
    return lax.dot_general(
        left, right, (((1,), (1,)), ((), ())), preferred_element_type=jnp.float32
    )


def nn(left, right):
    return jnp.dot(left, right, preferred_element_type=jnp.float32)


def flip(block, mask):
    size = lax.axis_size(AXES)
    return lax.ppermute(block, AXES, [(i, i ^ mask) for i in range(size)])


def block_index():
    return lax.axis_index("seq") * lax.axis_size("heads") + lax.axis_index("heads")


def in_vmem(array):
    return pltpu.with_memory_space_constraint(array, pltpu.VMEM)


def level_scales(width, tokens, count):
    base = 1.0 / math.sqrt(width * tokens)
    return [base] + [base / math.sqrt(2.0 ** (level - 1)) for level in range(1, count)]


def state_kernel(
    bits, scales, q_hbm, k_hbm, v_hbm, g_hbm, w_hbm,
    q_out, k_out, v_out, g_out, w_out, qt_out, kt_out, state_out, own_out, other_out, sems, w_sem,
):
    heads, tokens, width = q_out.shape
    half = heads // 2
    pairs = ((q_hbm, q_out), (k_hbm, k_out), (v_hbm, v_out), (g_hbm, g_out))
    w_copy = pltpu.make_async_copy(w_hbm, w_out, w_sem)
    copies = [
        [
            pltpu.make_async_copy(src.at[:, pl.ds(h * width, width)], dst.at[h], sems.at[i, h])
            for i, (src, dst) in enumerate(pairs)
        ]
        for h in range(heads)
    ]
    for copy in copies[0]:
        copy.start()
    w_copy.start()
    for group in copies[1:]:
        for copy in group:
            copy.start()
    place = block_index()
    low_bit = place & 1
    for h in range(heads):
        for copy in copies[h]:
            copy.wait()
        if h == 0:
            w_copy.wait()
        query_t = q_out[h].T
        key_t = k_out[h].T
        qt_out[h] = query_t
        kt_out[h] = key_t
        state = nn(key_t, v_out[h])
        state_out[h] = state.astype(LOW)
        query_f = query_t.astype(jnp.float32)
        scaled = [
            (w_out[h, pl.ds(level, 1), :] * query_f).astype(LOW) for level in range(2, bits + 1)
        ]
        grads = nn(jnp.concatenate(scaled, 0), g_out[h])
        mixed = []
        for level in range(2, bits + 1):
            upper = ((place >> (level - 1)) & 1) == 1
            row = (level - 2) * width
            mixed.append(jnp.where(upper, scales[level] * grads[row : row + width], state).astype(LOW))

        @pl.when(low_bit == h // half)
        def _():
            for i, block in enumerate(mixed):
                own_out[i * half + h % half] = block

        @pl.when(low_bit != h // half)
        def _():
            for i, block in enumerate(mixed):
                other_out[i * half + h % half] = block


def first_level_kernel(
    scale, g_ref, w_ref, qt_ref, state_ref, own_ref, other_ref, d1_out, near_out, far_out
):
    heads = g_ref.shape[0]
    half = heads // 2
    near_out[...] = own_ref[half:]
    far_out[...] = other_ref[half:]
    upper = (block_index() & 1) == 1
    for h in range(heads):
        scaled = (w_ref[h, pl.ds(1, 1), :] * qt_ref[h].astype(jnp.float32)).astype(LOW)
        state = state_ref[h]
        d1_out[h] = jnp.where(upper, (scale * nn(scaled, g_ref[h])).astype(LOW), state)


def near_head(scale, h, q_ref, k_ref, v_ref, g_ref, w_ref, kt_ref, nk_out, nv_out, local):
    width, tokens = kt_ref.shape[1:]
    rows = min(ROWS, tokens)
    factor = scale * w_ref[h, pl.ds(0, 1), :]
    back, weight = [], []
    for start in range(0, tokens, rows):
        left = tokens - start
        key = k_ref[h, start : start + rows, :]
        value = v_ref[h, start : start + rows, :]
        query = q_ref[h, start:, :]
        grad = g_ref[h, start:, :]
        scores = nt(key, query)
        dots = nt(value, grad)
        allowed = lax.broadcasted_iota(jnp.int32, (rows, left), 0) <= lax.broadcasted_iota(
            jnp.int32, (rows, left), 1
        )
        scores = jnp.where(allowed, scores, 0.0)
        dots = jnp.where(allowed, dots, 0.0)
        part = jnp.sum(scores * dots, axis=0, keepdims=True)
        now = factor[:, start:]
        grad_mix = (now * dots).astype(LOW)
        score_mix = (now * scores).astype(LOW)
        nk_out[local, start : start + rows, :] = nn(grad_mix, query)
        nv_out[local, start : start + rows, :] = nn(score_mix, grad)
        back.append(nn(kt_ref[h, :, start : start + rows], grad_mix))
        weight.append(scale * part)
    return back, weight


def store_sums(ref, h, rows, parts):
    tokens = parts[0].shape[1]
    for i, part in enumerate(parts):
        start = tokens - part.shape[1]
        if i == 0:
            ref[h, rows, :] = part
        else:
            ref[h, rows, start:] += part


def early_kernel(count, scale, *refs):
    ins, (d1_ref, nq_out, nk_out, nv_out, nw_out, d1_out) = refs[:6], refs[6:]
    d1_out[...] = d1_ref[...]
    for h in range(count):
        back, weight = near_head(scale, h, *ins, nk_out, nv_out, h)
        store_sums(nq_out, h, slice(None), back)
        store_sums(nw_out, h, slice(None), weight)


def late_kernel(count, scales, *refs):
    ins, refs = refs[:6], refs[6:]
    qt_ref, r1_ref, nq_ref, nw_ref, sum_out, gw_out, nk_out, nv_out = refs
    g_ref, w_ref = ins[3], ins[4]
    heads = sum_out.shape[0]
    upper = (block_index() & 1) == 1
    for h in range(heads):
        gw_out[h] = jnp.zeros(gw_out.shape[1:], jnp.float32)
        if h < count:
            sum_out[h] = nq_ref[h]
            gw_out[h, pl.ds(0, 1), :] = nw_ref[h]
        else:
            back, weight = near_head(scales[0], h, *ins, nk_out, nv_out, h - count)
            store_sums(sum_out, h, slice(None), back)
            store_sums(gw_out, h, pl.ds(0, 1), weight)
        add_level(scales[1], h, 1, jnp.where(upper, r1_ref[h], 0), g_ref, w_ref, qt_ref, sum_out, gw_out)


def add_level(scale, h, level, sibling, g_ref, w_ref, qt_ref, sum_ref, gw_ref):
    products = nt(sibling, g_ref[h])
    sum_ref[h] += (scale * w_ref[h, pl.ds(level, 1), :]) * products
    gw_ref[h, pl.ds(level, 1), :] = scale * jnp.sum(
        products * qt_ref[h].astype(jnp.float32), axis=0, keepdims=True
    )


def far_kernel(bits, scales, count, *refs):
    k_ref, v_ref, g_ref, w_ref, qt_ref, sum_ref, weight_ref, r1_ref = refs[:8]
    early, late, refs = refs[8:10], refs[10:12], refs[12:]
    own_refs, other_refs, refs = refs[: bits - 1], refs[bits - 1 : 2 * bits - 2], refs[2 * bits - 2 :]
    gq_hbm, gk_hbm, gv_hbm, gw_hbm, gq_buf, gk_buf, gv_buf, gw_buf, sems, w_sem = refs
    heads, tokens, width = k_ref.shape
    half = heads // 2
    place = block_index()
    low_bit = place & 1
    copies = []
    gw_buf[...] = weight_ref[...]
    for h in range(heads):
        nk_ref, nv_ref = early if h < count else late
        local = h if h < count else h - count
        grad = g_ref[h]
        query_t = qt_ref[h].astype(jnp.float32)
        reverse = jnp.where(low_bit == 1, 0, r1_ref[h]).astype(jnp.float32)
        total = sum_ref[h]
        for level in range(2, bits + 1):
            own_ref, other_ref = own_refs[level - 2], other_refs[level - 2]
            got = jnp.where(low_bit == h // half, own_ref[h % half], other_ref[h % half])
            upper = ((place >> (level - 1)) & 1) == 1
            sibling = jnp.where(upper, got, 0)
            reverse = reverse + jnp.where(upper, 0, got).astype(jnp.float32)
            products = nt(sibling, grad)
            total = total + (scales[level] * w_ref[h, pl.ds(level, 1), :]) * products
            gw_buf[h, pl.ds(level, 1), :] = scales[level] * jnp.sum(
                products * query_t, axis=0, keepdims=True
            )
        low = reverse.astype(LOW)
        gq_buf[h] = total.astype(LOW).T
        gk_buf[h] = (nk_ref[local] + nt(v_ref[h], low)).astype(LOW)
        gv_buf[h] = (nv_ref[local] + nn(k_ref[h], low)).astype(LOW)
        for i, (buf, hbm) in enumerate(((gq_buf, gq_hbm), (gk_buf, gk_hbm), (gv_buf, gv_hbm))):
            copy = pltpu.make_async_copy(buf.at[h], hbm.at[:, pl.ds(h * width, width)], sems.at[i, h])
            copy.start()
            copies.append(copy)
    copy = pltpu.make_async_copy(gw_buf, gw_hbm, w_sem)
    copy.start()
    copies.append(copy)
    for copy in copies:
        copy.wait()


ANY = pl.BlockSpec(memory_space=pl.ANY)
IN_VMEM = pl.BlockSpec(memory_space=pltpu.VMEM)
LIMIT = 16 * 1024 * 1024
EARLY = 1


def call(kernel, name, flops, out_shape, operands):
    outs = [pltpu.VMEM(shape, dtype) for shape, dtype in out_shape]
    return pl.pallas_call(
        kernel,
        out_shape=outs,
        in_specs=[IN_VMEM] * len(operands),
        out_specs=[IN_VMEM] * len(outs),
        compiler_params=pltpu.CompilerParams(vmem_limit_bytes=LIMIT),
        cost_estimate=pl.CostEstimate(flops=flops, bytes_accessed=0, transcendentals=0),
        name=name,
    )(*[in_vmem(x) for x in operands])


def on_device(queries, keys, values, out_grad, level_weights):
    tokens = queries.shape[0]
    heads, levels, _ = level_weights.shape
    width = queries.shape[1] // heads
    half = heads // 2
    bits = lax.axis_size(AXES).bit_length() - 1
    scales = level_scales(width, tokens, levels)
    by_head = pltpu.VMEM((heads, tokens, width), LOW)
    by_head_t = pltpu.VMEM((heads, width, tokens), LOW)
    halves = (bits - 1) * half
    f32 = jnp.float32
    near_flops = 1000 * tokens * tokens * width
    (q_v, k_v, v_v, g_v, w_v, qt, kt, state, own, other) = pl.pallas_call(
        functools.partial(state_kernel, bits, scales),
        out_shape=(
            by_head, by_head, by_head, by_head,
            pltpu.VMEM((heads, levels, tokens), jnp.float32),
            by_head_t, by_head_t,
            pltpu.VMEM((heads, width, width), LOW),
            pltpu.VMEM((halves, width, width), LOW),
            pltpu.VMEM((halves, width, width), LOW),
        ),
        in_specs=[ANY] * 5,
        out_specs=(IN_VMEM,) * 10,
        scratch_shapes=[pltpu.SemaphoreType.DMA((4, heads)), pltpu.SemaphoreType.DMA],
        compiler_params=pltpu.CompilerParams(vmem_limit_bytes=LIMIT),
        cost_estimate=pl.CostEstimate(
            flops=2 * heads * (bits + 1) * tokens * width * width,
            bytes_accessed=4 * heads * tokens * width * 2,
            transcendentals=0,
        ),
        name="states",
    )(*[pltpu.with_memory_space_constraint(x, pltpu.HBM) for x in (queries, keys, values, out_grad, level_weights)])
    got_x = flip(other, 1)
    rest = ((halves - half, width, width), LOW)
    full = ((heads, width, width), LOW)
    d1, mine, far = call(
        functools.partial(first_level_kernel, scales[1]), "first_level", near_flops,
        [full, rest, rest], [g_v, w_v, qt, state, own, other],
    )
    ins = [q_v, k_v, v_v, g_v, w_v, kt]
    nq, nk_a, nv_a, nw, d1 = call(
        functools.partial(early_kernel, EARLY, scales[0]), "near_early", near_flops,
        [
            ((EARLY, width, tokens), f32), ((EARLY, tokens, width), f32),
            ((EARLY, tokens, width), f32), ((EARLY, 1, tokens), f32), full,
        ],
        [*ins, d1],
    )
    got_1 = flip(d1, 1)
    got_z = flip(mine, 2)
    got_d = flip(far, 3)
    as_f = lambda x: x.astype(jnp.float32)
    pair = (as_f(own[:half]) + as_f(got_x[:half])).astype(LOW)
    quad = as_f(own[half:]) + as_f(got_x[half:]) + as_f(got_z) + as_f(got_d)
    sums = [pair]
    for bit in range(2, bits):
        sums.append(quad[:half].astype(LOW))
        quad = quad[half:]
        if bit < bits - 1:
            quad = quad + as_f(flip(quad.astype(LOW), 1 << bit))
    own_half = [flip(x, 1 << (i + 1)) for i, x in enumerate(sums)]
    other_half = [flip(x, (1 << (i + 1)) ^ 1) for i, x in enumerate(sums)]
    later = heads - EARLY
    total, weights, nk_b, nv_b = call(
        functools.partial(late_kernel, EARLY, scales), "near_late", near_flops,
        [
            ((heads, width, tokens), f32), ((heads, levels, tokens), f32),
            ((later, tokens, width), f32), ((later, tokens, width), f32),
        ],
        [*ins, qt, got_1, nq, nw],
    )
    operands = [k_v, v_v, g_v, w_v, qt, total, weights, got_1, nk_a, nv_a, nk_b, nv_b]
    operands += [*own_half, *other_half]
    out = jax.ShapeDtypeStruct((tokens, heads * width), LOW)
    return pl.pallas_call(
        functools.partial(far_kernel, bits, scales, EARLY),
        out_shape=(out, out, out, jax.ShapeDtypeStruct((heads, levels, tokens), jnp.float32)),
        in_specs=[IN_VMEM] * len(operands),
        out_specs=(ANY,) * 4,
        scratch_shapes=[pltpu.VMEM((heads, tokens, width), LOW)] * 3
        + [
            pltpu.VMEM((heads, levels, tokens), jnp.float32),
            pltpu.SemaphoreType.DMA((3, heads)),
            pltpu.SemaphoreType.DMA,
        ],
        compiler_params=pltpu.CompilerParams(vmem_limit_bytes=LIMIT),
        cost_estimate=pl.CostEstimate(
            flops=2 * heads * (bits + 2) * tokens * width * width,
            bytes_accessed=3 * heads * tokens * width * 2,
            transcendentals=0,
        ),
        name="far",
    )(*[in_vmem(x) for x in operands])


def solution(mesh):
    rows = P(("groups", "seq", "heads"), "sub")
    weights = P("sub", None, ("groups", "seq", "heads"))
    return jax.shard_map(
        on_device,
        mesh=mesh,
        in_specs=(rows, rows, rows, rows, weights),
        out_specs=(rows, rows, rows, weights),
        check_vma=False,
    )
```

```python
import functools
import math

import jax
import jax.numpy as jnp
from jax import lax
from jax.experimental import pallas as pl
from jax.experimental.pallas import tpu as pltpu
from jax.sharding import PartitionSpec as P

AXES = ("seq", "heads")
LOW = jnp.bfloat16
ROWS = 256


def nt(left, right):
    return lax.dot_general(
        left, right, (((1,), (1,)), ((), ())), preferred_element_type=jnp.float32
    )


def nn(left, right):
    return jnp.dot(left, right, preferred_element_type=jnp.float32)


def flip(block, mask):
    size = lax.axis_size(AXES)
    return lax.ppermute(block, AXES, [(i, i ^ mask) for i in range(size)])


def block_index():
    return lax.axis_index("seq") * lax.axis_size("heads") + lax.axis_index("heads")


def in_vmem(array):
    return pltpu.with_memory_space_constraint(array, pltpu.VMEM)


def level_scales(width, tokens, count):
    base = 1.0 / math.sqrt(width * tokens)
    return [base] + [base / math.sqrt(2.0 ** (level - 1)) for level in range(1, count)]


def top_kernel(
    bits, scales, q_hbm, k_hbm, v_hbm, g_hbm, w_hbm,
    q_out, k_out, v_out, g_out, w_out, t_out, own_out, other_out, sems, w_sem,
):
    heads, tokens, width = q_out.shape
    half = heads // 2
    pairs = ((q_hbm, q_out), (k_hbm, k_out), (v_hbm, v_out), (g_hbm, g_out))
    w_copy = pltpu.make_async_copy(w_hbm, w_out, w_sem)
    q_copy, k_copy, v_copy, g_copy = [
        [
            pltpu.make_async_copy(src.at[:, pl.ds(h * width, width)], dst.at[h], sems.at[i, h])
            for h in range(heads)
        ]
        for i, (src, dst) in enumerate(pairs)
    ]
    place = block_index()
    low_bit = place & 1

    def start(*groups):
        for h in range(heads):
            for group in groups:
                group[h].start()

    def wait(*groups):
        for h in range(heads):
            for group in groups:
                group[h].wait()

    def states(level, upper, left_copy, right_copy):
        left_ref, right_ref = (q_out, g_out) if upper else (k_out, v_out)
        for h in range(heads):
            if left_copy is not None:
                left_copy[h].wait()
                right_copy[h].wait()
            turned = left_ref[h].T
            if level == bits:
                t_out[h] = turned
            if upper:
                scaled = (w_out[h, pl.ds(level, 1), :] * turned.astype(jnp.float32)).astype(LOW)
                state = scales[level] * nn(scaled, right_ref[h])
            else:
                state = nn(turned, right_ref[h])
            state = state.astype(LOW)
            row = (level - 3) * half + h % half

            @pl.when(low_bit == h // half)
            def _():
                own_out[row] = state

            @pl.when(low_bit != h // half)
            def _():
                other_out[row] = state

    top = (place >> (bits - 1)) & 1

    @pl.when(top == 1)
    def _():
        w_copy.start()
        start(q_copy, g_copy)
        start(k_copy, v_copy)
        w_copy.wait()
        states(bits, True, q_copy, g_copy)
        wait(k_copy, v_copy)

    @pl.when(top == 0)
    def _():
        start(k_copy, v_copy)
        w_copy.start()
        start(q_copy, g_copy)
        states(bits, False, k_copy, v_copy)
        w_copy.wait()
        wait(q_copy, g_copy)

    for level in range(3, bits):
        bit = (place >> (level - 1)) & 1
        for value in (0, 1):

            @pl.when(bit == value)
            def _():
                states(level, value == 1, None, None)


def low_kernel(
    bits, scales, q_ref, k_ref, v_ref, g_ref, w_ref, t_ref, qt_out, kt_out, d1_out, d2_out
):
    heads = q_ref.shape[0]
    place = block_index()
    top = ((place >> (bits - 1)) & 1) == 1
    for h in range(heads):
        turned = t_ref[h]
        other = jnp.where(top, k_ref[h], q_ref[h]).T
        query_t = jnp.where(top, turned, other)
        key_t = jnp.where(top, other, turned)
        qt_out[h] = query_t
        kt_out[h] = key_t
        for level, out in ((1, d1_out), (2, d2_out)):
            upper = ((place >> (level - 1)) & 1) == 1
            scaled = (w_ref[h, pl.ds(level, 1), :] * query_t.astype(jnp.float32)).astype(LOW)
            left = jnp.where(upper, scaled, key_t)
            right = jnp.where(upper, g_ref[h], v_ref[h])
            out[h] = (jnp.where(upper, scales[level], 1.0) * nn(left, right)).astype(LOW)


def near_head(scale, h, q_ref, k_ref, v_ref, g_ref, w_ref, kt_ref, nk_out, nv_out, local):
    width, tokens = kt_ref.shape[1:]
    rows = min(ROWS, tokens)
    factor = scale * w_ref[h, pl.ds(0, 1), :]
    back, weight = [], []
    for start in range(0, tokens, rows):
        left = tokens - start
        key = k_ref[h, start : start + rows, :]
        value = v_ref[h, start : start + rows, :]
        query = q_ref[h, start:, :]
        grad = g_ref[h, start:, :]
        scores = nt(key, query)
        dots = nt(value, grad)
        allowed = lax.broadcasted_iota(jnp.int32, (rows, left), 0) <= lax.broadcasted_iota(
            jnp.int32, (rows, left), 1
        )
        scores = jnp.where(allowed, scores, 0.0)
        dots = jnp.where(allowed, dots, 0.0)
        part = jnp.sum(scores * dots, axis=0, keepdims=True)
        now = factor[:, start:]
        grad_mix = (now * dots).astype(LOW)
        score_mix = (now * scores).astype(LOW)
        nk_out[local, start : start + rows, :] = nn(grad_mix, query)
        nv_out[local, start : start + rows, :] = nn(score_mix, grad)
        back.append(nn(kt_ref[h, :, start : start + rows], grad_mix))
        weight.append(scale * part)
    return back, weight


def store_sums(ref, h, rows, parts):
    tokens = parts[0].shape[1]
    for i, part in enumerate(parts):
        start = tokens - part.shape[1]
        if i == 0:
            ref[h, rows, :] = part
        else:
            ref[h, rows, start:] += part


def near_kernel(scales, *refs):
    ins, (qt_ref, r1_ref, sum_out, gw_out, nk_out, nv_out) = refs[:6], refs[6:]
    g_ref, w_ref = ins[3], ins[4]
    upper = (block_index() & 1) == 1
    for h in range(sum_out.shape[0]):
        gw_out[h] = jnp.zeros(gw_out.shape[1:], jnp.float32)
        back, weight = near_head(scales[0], h, *ins, nk_out, nv_out, h)
        store_sums(sum_out, h, slice(None), back)
        store_sums(gw_out, h, pl.ds(0, 1), weight)
        products = nt(jnp.where(upper, r1_ref[h], 0), g_ref[h])
        sum_out[h] += (scales[1] * w_ref[h, pl.ds(1, 1), :]) * products
        gw_out[h, pl.ds(1, 1), :] = scales[1] * jnp.sum(
            products * qt_ref[h].astype(jnp.float32), axis=0, keepdims=True
        )


def far_kernel(bits, scales, *refs):
    k_ref, v_ref, g_ref, w_ref, qt_ref, sum_ref, weight_ref, nk_ref, nv_ref = refs[:9]
    (r1_ref, z2_ref, d2_ref), refs = refs[9:12], refs[12:]
    own_refs, other_refs, refs = refs[: bits - 2], refs[bits - 2 : 2 * bits - 4], refs[2 * bits - 4 :]
    gq_hbm, gk_hbm, gv_hbm, gw_hbm, gq_buf, gk_buf, gv_buf, gw_buf, sems, w_sem = refs
    heads, tokens, width = k_ref.shape
    half = heads // 2
    place = block_index()
    low_bit = place & 1
    copies = []
    gw_buf[...] = weight_ref[...]
    for h in range(heads):
        grad = g_ref[h]
        query_t = qt_ref[h].astype(jnp.float32)
        reverse = jnp.where(low_bit == 1, 0, r1_ref[h]).astype(jnp.float32)
        total = sum_ref[h]
        for level in range(2, bits + 1):
            if level == 2:
                got = z2_ref[h].astype(jnp.float32) + d2_ref[h].astype(jnp.float32)
            else:
                own_ref, other_ref = own_refs[level - 3], other_refs[level - 3]
                got = jnp.where(low_bit == h // half, own_ref[h % half], other_ref[h % half])
            upper = ((place >> (level - 1)) & 1) == 1
            sibling = jnp.where(upper, got, 0).astype(LOW)
            reverse = reverse + jnp.where(upper, 0, got).astype(jnp.float32)
            products = nt(sibling, grad)
            total = total + (scales[level] * w_ref[h, pl.ds(level, 1), :]) * products
            gw_buf[h, pl.ds(level, 1), :] = scales[level] * jnp.sum(
                products * query_t, axis=0, keepdims=True
            )
        low = reverse.astype(LOW)
        gq_buf[h] = total.astype(LOW).T
        gk_buf[h] = (nk_ref[h] + nt(v_ref[h], low)).astype(LOW)
        gv_buf[h] = (nv_ref[h] + nn(k_ref[h], low)).astype(LOW)
        for i, (buf, hbm) in enumerate(((gq_buf, gq_hbm), (gk_buf, gk_hbm), (gv_buf, gv_hbm))):
            copy = pltpu.make_async_copy(buf.at[h], hbm.at[:, pl.ds(h * width, width)], sems.at[i, h])
            copy.start()
            copies.append(copy)
    copy = pltpu.make_async_copy(gw_buf, gw_hbm, w_sem)
    copy.start()
    copies.append(copy)
    for copy in copies:
        copy.wait()


ANY = pl.BlockSpec(memory_space=pl.ANY)
IN_VMEM = pl.BlockSpec(memory_space=pltpu.VMEM)
LIMIT = 16 * 1024 * 1024


def in_hbm(array):
    return pltpu.with_memory_space_constraint(array, pltpu.HBM)


def call(kernel, name, flops, out_shape, operands):
    outs = [pltpu.VMEM(shape, dtype) for shape, dtype in out_shape]
    return pl.pallas_call(
        kernel,
        out_shape=outs,
        in_specs=[IN_VMEM] * len(operands),
        out_specs=[IN_VMEM] * len(outs),
        compiler_params=pltpu.CompilerParams(vmem_limit_bytes=LIMIT),
        cost_estimate=pl.CostEstimate(flops=flops, bytes_accessed=0, transcendentals=0),
        name=name,
    )(*[in_vmem(x) for x in operands])


def on_device(queries, keys, values, out_grad, level_weights):
    tokens = queries.shape[0]
    heads, levels, _ = level_weights.shape
    width = queries.shape[1] // heads
    half = heads // 2
    bits = lax.axis_size(AXES).bit_length() - 1
    scales = level_scales(width, tokens, levels)
    f32 = jnp.float32
    cost = 1000 * tokens * tokens * width
    by_head = ((heads, tokens, width), LOW)
    turned = ((heads, width, tokens), LOW)
    full = ((heads, width, width), LOW)
    halves = (((bits - 2) * half, width, width), LOW)
    weight_rows = ((heads, levels, tokens), f32)
    outs = [by_head] * 4 + [weight_rows, turned, halves, halves]
    q_v, k_v, v_v, g_v, w_v, t_v, own, other = pl.pallas_call(
        functools.partial(top_kernel, bits, scales),
        out_shape=[pltpu.VMEM(shape, dtype) for shape, dtype in outs],
        in_specs=[ANY] * 5,
        out_specs=[IN_VMEM] * len(outs),
        scratch_shapes=[pltpu.SemaphoreType.DMA((4, heads)), pltpu.SemaphoreType.DMA],
        compiler_params=pltpu.CompilerParams(vmem_limit_bytes=LIMIT),
        cost_estimate=pl.CostEstimate(flops=cost, bytes_accessed=0, transcendentals=0),
        name="top_states",
    )(*[in_hbm(x) for x in (queries, keys, values, out_grad, level_weights)])

    def as_f(array):
        return array.astype(f32)

    got_x = flip(other, 1)
    got_z = flip(own, 2)
    got_d = flip(other, 3)
    quad = as_f(own) + as_f(got_x) + as_f(got_z) + as_f(got_d)
    qt, kt, d1, d2 = call(
        functools.partial(low_kernel, bits, scales), "low_states", cost,
        [turned, turned, full, full], [q_v, k_v, v_v, g_v, w_v, t_v],
    )
    got_1 = flip(d1, 1)
    got_2 = flip(d2, 2)
    sums = []
    for bit in range(2, bits):
        sums.append(quad[:half].astype(LOW))
        quad = quad[half:]
        if bit < bits - 1:
            quad = quad + as_f(flip(quad.astype(LOW), 1 << bit))
    own_half = [flip(x, 1 << (i + 2)) for i, x in enumerate(sums)]
    other_half = [flip(x, (1 << (i + 2)) ^ 1) for i, x in enumerate(sums)]
    diagonal_2 = flip(got_2, 1)
    total, weights, near_k, near_v = call(
        functools.partial(near_kernel, scales), "near", cost,
        [((heads, width, tokens), f32), weight_rows, *[((heads, tokens, width), f32)] * 2],
        [q_v, k_v, v_v, g_v, w_v, kt, qt, got_1],
    )
    operands = [k_v, v_v, g_v, w_v, qt, total, weights, near_k, near_v]
    operands += [got_1, got_2, diagonal_2, *own_half, *other_half]
    out = jax.ShapeDtypeStruct((tokens, heads * width), LOW)
    return pl.pallas_call(
        functools.partial(far_kernel, bits, scales),
        out_shape=(out, out, out, jax.ShapeDtypeStruct((heads, levels, tokens), f32)),
        in_specs=[IN_VMEM] * len(operands),
        out_specs=(ANY,) * 4,
        scratch_shapes=[pltpu.VMEM((heads, tokens, width), LOW)] * 3
        + [
            pltpu.VMEM((heads, levels, tokens), f32),
            pltpu.SemaphoreType.DMA((3, heads)),
            pltpu.SemaphoreType.DMA,
        ],
        compiler_params=pltpu.CompilerParams(vmem_limit_bytes=LIMIT),
        cost_estimate=pl.CostEstimate(flops=cost, bytes_accessed=0, transcendentals=0),
        name="far",
    )(*[in_vmem(x) for x in operands])


def solution(mesh):
    rows = P(("groups", "seq", "heads"), "sub")
    weights = P("sub", None, ("groups", "seq", "heads"))
    return jax.shard_map(
        on_device,
        mesh=mesh,
        in_specs=(rows, rows, rows, rows, weights),
        out_specs=(rows, rows, rows, weights),
        check_vma=False,
    )
```

```python
import functools
import math

import jax
import jax.numpy as jnp
from jax import lax
from jax.experimental import pallas as pl
from jax.experimental.pallas import tpu as pltpu
from jax.sharding import PartitionSpec as P

AXES = ("seq", "heads")
LOW = jnp.bfloat16
ROWS = 256
GROUP = 2


def nt(left, right):
    return lax.dot_general(
        left, right, (((1,), (1,)), ((), ())), preferred_element_type=jnp.float32
    )


def nn(left, right):
    return jnp.dot(left, right, preferred_element_type=jnp.float32)


def flip(block, mask):
    size = lax.axis_size(AXES)
    return lax.ppermute(block, AXES, [(i, i ^ mask) for i in range(size)])


def block_index():
    return lax.axis_index("seq") * lax.axis_size("heads") + lax.axis_index("heads")


def head(ref, h, width, rows=slice(None)):
    return ref[rows, h * width : (h + 1) * width]


def in_vmem(array):
    return pltpu.with_memory_space_constraint(array, pltpu.VMEM)


def level_scales(width, tokens, count):
    base = 1.0 / math.sqrt(width * tokens)
    return [base] + [base / math.sqrt(2.0 ** (level - 1)) for level in range(1, count)]


def top_kernel(bits, scales, q_hbm, k_hbm, v_hbm, g_hbm, w_hbm, t_out, own_out, other_out, left_buf, right_buf, w_buf, sems):
    rows, heads, tokens, width = left_buf.shape
    half = heads // 2
    place = block_index()
    low_bit = place & 1

    def states(index, upper):
        level = index + 3
        for first in range(0, heads, GROUP):
            lefts, rights = [], []
            for h in range(first, first + GROUP):
                for copy in copies(index, h, upper):
                    copy.wait()
                turned = left_buf[index, h].T
                if level == bits:
                    t_out[h] = turned
                if upper:
                    turned = (w_buf[index, h] * turned.astype(jnp.float32)).astype(LOW)
                lefts.append(turned)
                rights.append(right_buf[index, h])
            product = nn(jnp.concatenate(lefts, 0), jnp.concatenate(rights, 1))
            for i in range(GROUP):
                h = first + i
                part = slice(i * width, i * width + width)
                state = product[part, part]
                if upper:
                    state = scales[level] * state
                state = state.astype(LOW)
                row = index * half + h % half

                @pl.when(low_bit == h // half)
                def _():
                    own_out[row] = state

                @pl.when(low_bit != h // half)
                def _():
                    other_out[row] = state

    def copies(index, h, upper):
        left, right = (q_hbm, g_hbm) if upper else (k_hbm, v_hbm)
        columns = pl.ds(h * width, width)
        made = [
            pltpu.make_async_copy(left.at[:, columns], left_buf.at[index, h], sems.at[0, index, h]),
            pltpu.make_async_copy(right.at[:, columns], right_buf.at[index, h], sems.at[1, index, h]),
        ]
        if upper:
            row = w_hbm.at[h, pl.ds(index + 3, 1), :]
            made.append(pltpu.make_async_copy(row, w_buf.at[index, h], sems.at[2, index, h]))
        return made

    for index in range(rows):
        bit = (place >> (index + 2)) & 1
        for value in (0, 1):

            @pl.when(bit == value)
            def _():
                for h in range(heads):
                    for copy in copies(index, h, value == 1):
                        copy.start()
                states(index, value == 1)


def low_kernel(
    bits, scales, q_ref, k_ref, v_ref, g_ref, w_ref, t_ref, qt_out, kt_out, d1_out, d2_out
):
    heads, width = t_ref.shape[:2]
    place = block_index()
    top = ((place >> (bits - 1)) & 1) == 1
    for h in range(heads):
        turned = t_ref[h]
        other = jnp.where(top, head(k_ref, h, width), head(q_ref, h, width)).T
        query_t = jnp.where(top, turned, other)
        key_t = jnp.where(top, other, turned)
        qt_out[h] = query_t
        kt_out[h] = key_t
        for level, out in ((1, d1_out), (2, d2_out)):
            upper = ((place >> (level - 1)) & 1) == 1
            scaled = (w_ref[h, pl.ds(level, 1), :] * query_t.astype(jnp.float32)).astype(LOW)
            left = jnp.where(upper, scaled, key_t)
            right = jnp.where(upper, head(g_ref, h, width), head(v_ref, h, width))
            out[h] = (jnp.where(upper, scales[level], 1.0) * nn(left, right)).astype(LOW)


def near_head(scale, h, q_ref, k_ref, v_ref, g_ref, w_ref, kt_ref, nk_out, nv_out, local):
    width, tokens = kt_ref.shape[1:]
    rows = min(ROWS, tokens)
    factor = scale * w_ref[h, pl.ds(0, 1), :]
    back, weight = [], []
    for start in range(0, tokens, rows):
        left = tokens - start
        key = head(k_ref, h, width, slice(start, start + rows))
        value = head(v_ref, h, width, slice(start, start + rows))
        query = head(q_ref, h, width, slice(start, None))
        grad = head(g_ref, h, width, slice(start, None))
        scores = nt(key, query)
        dots = nt(value, grad)
        allowed = lax.broadcasted_iota(jnp.int32, (rows, left), 0) <= lax.broadcasted_iota(
            jnp.int32, (rows, left), 1
        )
        scores = jnp.where(allowed, scores, 0.0)
        dots = jnp.where(allowed, dots, 0.0)
        part = jnp.sum(scores * dots, axis=0, keepdims=True)
        now = factor[:, start:]
        grad_mix = (now * dots).astype(LOW)
        score_mix = (now * scores).astype(LOW)
        nk_out[local, start : start + rows, :] = nn(grad_mix, query)
        nv_out[local, start : start + rows, :] = nn(score_mix, grad)
        back.append(nn(kt_ref[h, :, start : start + rows], grad_mix))
        weight.append(scale * part)
    return back, weight


def store_sums(ref, h, rows, parts):
    tokens = parts[0].shape[1]
    for i, part in enumerate(parts):
        start = tokens - part.shape[1]
        if i == 0:
            ref[h, rows, :] = part
        else:
            ref[h, rows, start:] += part


def near_kernel(scales, *refs):
    ins, (qt_ref, r1_ref, sum_out, gw_out, nk_out, nv_out) = refs[:6], refs[6:]
    g_ref, w_ref = ins[3], ins[4]
    upper = (block_index() & 1) == 1
    for h in range(sum_out.shape[0]):
        gw_out[h] = jnp.zeros(gw_out.shape[1:], jnp.float32)
        back, weight = near_head(scales[0], h, *ins, nk_out, nv_out, h)
        store_sums(sum_out, h, slice(None), back)
        store_sums(gw_out, h, pl.ds(0, 1), weight)
        products = nt(jnp.where(upper, r1_ref[h], 0), head(g_ref, h, sum_out.shape[1]))
        sum_out[h] += (scales[1] * w_ref[h, pl.ds(1, 1), :]) * products
        gw_out[h, pl.ds(1, 1), :] = scales[1] * jnp.sum(
            products * qt_ref[h].astype(jnp.float32), axis=0, keepdims=True
        )


def spread(blocks):
    zeros = jnp.zeros_like(blocks[0])
    return jnp.concatenate(
        [
            jnp.concatenate([block if i == j else zeros for j in range(len(blocks))], 1)
            for i, block in enumerate(blocks)
        ],
        0,
    )


def far_kernel(bits, scales, *refs):
    k_ref, v_ref, g_ref, w_ref, qt_ref, _, weight_ref, nk_ref, nv_ref = refs[:9]
    (r1_ref, z2_ref, d2_ref), refs = refs[9:12], refs[12:]
    own_refs, other_refs, refs = refs[: bits - 2], refs[bits - 2 : 2 * bits - 4], refs[2 * bits - 4 :]
    gq_hbm, gk_hbm, gv_hbm, gw_hbm, sum_ref, gq_buf, gk_buf, gv_buf, gw_buf, sems, w_sem = refs
    heads, width, tokens = sum_ref.shape
    half = heads // 2
    place = block_index()
    low_bit = place & 1
    copies = []

    def is_upper(level):
        return ((place >> (level - 1)) & 1) == 1

    def received(level, h):
        if level == 1:
            return r1_ref[h]
        if level == 2:
            return z2_ref[h].astype(jnp.float32) + d2_ref[h].astype(jnp.float32)
        own_ref, other_ref = own_refs[level - 3], other_refs[level - 3]
        return jnp.where(low_bit == h // half, own_ref[h % half], other_ref[h % half])

    def send(i, first, buf, hbm):
        span = pl.ds(first * width, GROUP * width)
        copy = pltpu.make_async_copy(buf.at[first // GROUP], hbm.at[:, span], sems.at[i, first])
        copy.start()
        copies.append(copy)

    gw_buf[...] = weight_ref[...]
    for first in range(0, heads, GROUP):
        group = range(first, first + GROUP)
        reverses = []
        for h in group:
            total = jnp.zeros((width, width), jnp.float32)
            for level in range(1, bits + 1):
                total = total + jnp.where(is_upper(level), 0, received(level, h)).astype(jnp.float32)
            reverses.append(total.astype(LOW))
        low = spread(reverses)
        near_k = jnp.concatenate([nk_ref[h] for h in group], 1)
        near_v = jnp.concatenate([nv_ref[h] for h in group], 1)
        value = v_ref[:, first * width : (first + GROUP) * width]
        key = k_ref[:, first * width : (first + GROUP) * width]
        gk_buf[first // GROUP] = (near_k + nt(value, low)).astype(LOW)
        gv_buf[first // GROUP] = (near_v + nn(key, low)).astype(LOW)
        send(0, first, gk_buf, gk_hbm)
        send(1, first, gv_buf, gv_hbm)
    for level in range(2, bits + 1):

        @pl.when(is_upper(level))
        def _():
            for first in range(0, heads, GROUP):
                group = range(first, first + GROUP)
                siblings = spread([received(level, h).astype(LOW) for h in group])
                products = nt(siblings, g_ref[:, first * width : (first + GROUP) * width])
                for i, h in enumerate(group):
                    mine = products[i * width : i * width + width]
                    sum_ref[h] += (scales[level] * w_ref[h, pl.ds(level, 1), :]) * mine
                    gw_buf[h, pl.ds(level, 1), :] = scales[level] * jnp.sum(
                        mine * qt_ref[h].astype(jnp.float32), axis=0, keepdims=True
                    )

    copy = pltpu.make_async_copy(gw_buf, gw_hbm, w_sem)
    copy.start()
    copies.append(copy)
    for first in range(0, heads, GROUP):
        for i in range(GROUP):
            gq_buf[first // GROUP, :, i * width : i * width + width] = sum_ref[first + i].astype(LOW).T
        send(2, first, gq_buf, gq_hbm)
    for copy in copies:
        copy.wait()


ANY = pl.BlockSpec(memory_space=pl.ANY)
IN_VMEM = pl.BlockSpec(memory_space=pltpu.VMEM)
LIMIT = 16 * 1024 * 1024


def in_hbm(array):
    return pltpu.with_memory_space_constraint(array, pltpu.HBM)


def call(kernel, name, flops, out_shape, operands):
    outs = [pltpu.VMEM(shape, dtype) for shape, dtype in out_shape]
    return pl.pallas_call(
        kernel,
        out_shape=outs,
        in_specs=[IN_VMEM] * len(operands),
        out_specs=[IN_VMEM] * len(outs),
        compiler_params=pltpu.CompilerParams(vmem_limit_bytes=LIMIT),
        cost_estimate=pl.CostEstimate(flops=flops, bytes_accessed=0, transcendentals=0),
        name=name,
    )(*[in_vmem(x) for x in operands])


def on_device(queries, keys, values, out_grad, level_weights):
    tokens = queries.shape[0]
    heads, levels, _ = level_weights.shape
    width = queries.shape[1] // heads
    half = heads // 2
    bits = lax.axis_size(AXES).bit_length() - 1
    scales = level_scales(width, tokens, levels)
    f32 = jnp.float32
    cost = 1000 * tokens * tokens * width
    turned = ((heads, width, tokens), LOW)
    full = ((heads, width, width), LOW)
    halves = (((bits - 2) * half, width, width), LOW)
    weight_rows = ((heads, levels, tokens), f32)
    outs = [turned, halves, halves]
    chosen = pltpu.VMEM((bits - 2, heads, tokens, width), LOW)
    t_v, own, other = pl.pallas_call(
        functools.partial(top_kernel, bits, scales),
        out_shape=[pltpu.VMEM(shape, dtype) for shape, dtype in outs],
        in_specs=[ANY] * 5,
        out_specs=[IN_VMEM] * len(outs),
        scratch_shapes=[
            chosen, chosen, pltpu.VMEM((bits - 2, heads, 1, tokens), f32),
            pltpu.SemaphoreType.DMA((3, bits - 2, heads)),
        ],
        compiler_params=pltpu.CompilerParams(vmem_limit_bytes=LIMIT),
        cost_estimate=pl.CostEstimate(flops=cost, bytes_accessed=0, transcendentals=0),
        name="top_states",
    )(*[in_hbm(x) for x in (queries, keys, values, out_grad, level_weights)])
    q_v, k_v, v_v, g_v, w_v = queries, keys, values, out_grad, level_weights

    def as_f(array):
        return array.astype(f32)

    got_x = flip(other, 1)
    got_z = flip(own, 2)
    got_d = flip(other, 3)
    quad = as_f(own) + as_f(got_x) + as_f(got_z) + as_f(got_d)
    qt, kt, d1, d2 = call(
        functools.partial(low_kernel, bits, scales), "low_states", cost,
        [turned, turned, full, full], [q_v, k_v, v_v, g_v, w_v, t_v],
    )
    got_1 = flip(d1, 1)
    got_2 = flip(d2, 2)
    sums = []
    for bit in range(2, bits):
        sums.append(quad[:half].astype(LOW))
        quad = quad[half:]
        if bit < bits - 1:
            quad = quad + as_f(flip(quad.astype(LOW), 1 << bit))
    own_half = [flip(x, 1 << (i + 2)) for i, x in enumerate(sums)]
    other_half = [flip(x, (1 << (i + 2)) ^ 1) for i, x in enumerate(sums)]
    diagonal_2 = flip(got_2, 1)
    total, weights, near_k, near_v = call(
        functools.partial(near_kernel, scales), "near", cost,
        [((heads, width, tokens), f32), weight_rows, *[((heads, tokens, width), f32)] * 2],
        [q_v, k_v, v_v, g_v, w_v, kt, qt, got_1],
    )
    operands = [k_v, v_v, g_v, w_v, qt, total, weights, near_k, near_v]
    operands += [got_1, got_2, diagonal_2, *own_half, *other_half]
    out = jax.ShapeDtypeStruct((tokens, heads * width), LOW)
    return pl.pallas_call(
        functools.partial(far_kernel, bits, scales),
        out_shape=(out, out, out, jax.ShapeDtypeStruct((heads, levels, tokens), f32), pltpu.VMEM((heads, width, tokens), f32)),
        in_specs=[IN_VMEM] * len(operands),
        out_specs=(ANY,) * 4 + (IN_VMEM,),
        input_output_aliases={5: 4},
        scratch_shapes=[pltpu.VMEM((heads // GROUP, tokens, GROUP * width), LOW)] * 3
        + [
            pltpu.VMEM((heads, levels, tokens), f32),
            pltpu.SemaphoreType.DMA((3, heads)),
            pltpu.SemaphoreType.DMA,
        ],
        compiler_params=pltpu.CompilerParams(vmem_limit_bytes=LIMIT),
        cost_estimate=pl.CostEstimate(flops=cost, bytes_accessed=0, transcendentals=0),
        name="far",
    )(*[in_vmem(x) for x in operands])[:4]


def solution(mesh):
    rows = P(("groups", "seq", "heads"), "sub")
    weights = P("sub", None, ("groups", "seq", "heads"))
    return jax.shard_map(
        on_device,
        mesh=mesh,
        in_specs=(rows, rows, rows, rows, weights),
        out_specs=(rows, rows, rows, weights),
        check_vma=False,
    )
```

```python
import functools
import math

import jax
import jax.numpy as jnp
from jax import lax
from jax.experimental import pallas as pl
from jax.experimental.pallas import tpu as pltpu
from jax.sharding import PartitionSpec as P

AXES = ("seq", "heads")
LOW = jnp.bfloat16
ROWS = 256
GROUP = 2
CHUNKS = 1


def nt(left, right):
    return lax.dot_general(
        left, right, (((1,), (1,)), ((), ())), preferred_element_type=jnp.float32
    )


def nn(left, right):
    return jnp.dot(left, right, preferred_element_type=jnp.float32)


def flip(block, mask):
    size = lax.axis_size(AXES)
    return lax.ppermute(block, AXES, [(i, i ^ mask) for i in range(size)])


def swap_halves(block, bit, upper_turns):
    routes = []
    for i in range(lax.axis_size(AXES)):
        upper = (i >> bit) & 1 == 1
        routes.append((i, i ^ (1 << bit) ^ (1 if upper == upper_turns else 0)))
    return lax.ppermute(block, AXES, routes)


def block_index():
    return lax.axis_index("seq") * lax.axis_size("heads") + lax.axis_index("heads")


def head(ref, h, width, rows=slice(None)):
    return ref[rows, h * width : (h + 1) * width]


def in_vmem(array):
    return pltpu.with_memory_space_constraint(array, pltpu.VMEM)


def level_scales(width, tokens, count):
    base = 1.0 / math.sqrt(width * tokens)
    return [base] + [base / math.sqrt(2.0 ** (level - 1)) for level in range(1, count)]


def top_kernel(
    bits, scales, q_hbm, k_hbm, v_hbm, g_hbm, w_hbm, t_out, own_out, other_out, left_buf, right_buf, w_buf, sems
):
    heads, width, tokens = t_out.shape
    half = heads // 2
    span = tokens // CHUNKS
    place = block_index()
    low_bit = place & 1

    def copies(index, upper):
        left, right = (q_hbm, g_hbm) if upper else (k_hbm, v_hbm)
        made = []
        for chunk in range(CHUNKS):
            rows = pl.ds(chunk * span, span)
            made.append(
                [
                    pltpu.make_async_copy(left.at[rows], left_buf.at[index, rows], sems.at[0, index, chunk]),
                    pltpu.make_async_copy(right.at[rows], right_buf.at[index, rows], sems.at[1, index, chunk]),
                ]
            )
        if upper:
            level_row = w_hbm.at[:, pl.ds(index + 3, 1), :]
            made[0].append(pltpu.make_async_copy(level_row, w_buf.at[index], sems.at[2, index, 0]))
        return made

    def states(index, upper):
        level = index + 3
        made = copies(index, upper)
        for group in made:
            for copy in group:
                copy.start()
        totals = [None] * (heads // GROUP)
        for chunk, group in enumerate(made):
            for copy in group:
                copy.wait()
            rows = slice(chunk * span, chunk * span + span)
            for pair in range(heads // GROUP):
                lefts = []
                for h in range(pair * GROUP, pair * GROUP + GROUP):
                    turned = left_buf[index, rows, h * width : (h + 1) * width].T
                    if level == bits:
                        t_out[h, :, rows] = turned
                    if upper:
                        turned = (w_buf[index, h, :, rows] * turned.astype(jnp.float32)).astype(LOW)
                    lefts.append(turned)
                columns = slice(pair * GROUP * width, (pair + 1) * GROUP * width)
                part = nn(jnp.concatenate(lefts, 0), right_buf[index, rows, columns])
                totals[pair] = part if totals[pair] is None else totals[pair] + part
        for h in range(heads):
            block = slice(h % GROUP * width, h % GROUP * width + width)
            state = totals[h // GROUP][block, block]
            if upper:
                state = scales[level] * state
            state = state.astype(LOW)
            row = index * half + h % half

            @pl.when(low_bit == h // half)
            def _():
                own_out[row] = state

            @pl.when(low_bit != h // half)
            def _():
                other_out[row] = state

    for index in range(bits - 2):
        bit = (place >> (index + 2)) & 1
        for value in (0, 1):

            @pl.when(bit == value)
            def _():
                states(index, value == 1)


def mixed_state(level, scale, h, place, query_t, key_t, w_ref, v_ref, g_ref):
    width = query_t.shape[0]
    upper = ((place >> (level - 1)) & 1) == 1
    scaled = (w_ref[h, pl.ds(level, 1), :] * query_t.astype(jnp.float32)).astype(LOW)
    left = jnp.where(upper, scaled, key_t)
    right = jnp.where(upper, head(g_ref, h, width), head(v_ref, h, width))
    return (jnp.where(upper, scale, 1.0) * nn(left, right)).astype(LOW)


def second_kernel(bits, scale, q_ref, k_ref, v_ref, g_ref, w_ref, t_ref, qt_out, kt_out, d2_out):
    heads, width = t_ref.shape[:2]
    place = block_index()
    top = ((place >> (bits - 1)) & 1) == 1
    for h in range(heads):
        turned = t_ref[h]
        other = jnp.where(top, head(k_ref, h, width), head(q_ref, h, width)).T
        query_t = jnp.where(top, turned, other)
        key_t = jnp.where(top, other, turned)
        qt_out[h] = query_t
        kt_out[h] = key_t
        d2_out[h] = mixed_state(2, scale, h, place, query_t, key_t, w_ref, v_ref, g_ref)


def first_kernel(scale, v_ref, g_ref, w_ref, qt_ref, kt_ref, d1_out):
    place = block_index()
    for h in range(qt_ref.shape[0]):
        d1_out[h] = mixed_state(1, scale, h, place, qt_ref[h], kt_ref[h], w_ref, v_ref, g_ref)


def near_head(scale, h, q_ref, k_ref, v_ref, g_ref, w_ref, kt_ref, nk_out, nv_out, local):
    width, tokens = kt_ref.shape[1:]
    rows = min(ROWS, tokens)
    factor = scale * w_ref[h, pl.ds(0, 1), :]
    back, weight = [], []
    for start in range(0, tokens, rows):
        left = tokens - start
        key = head(k_ref, h, width, slice(start, start + rows))
        value = head(v_ref, h, width, slice(start, start + rows))
        query = head(q_ref, h, width, slice(start, None))
        grad = head(g_ref, h, width, slice(start, None))
        scores = nt(key, query)
        dots = nt(value, grad)
        allowed = lax.broadcasted_iota(jnp.int32, (rows, left), 0) <= lax.broadcasted_iota(
            jnp.int32, (rows, left), 1
        )
        scores = jnp.where(allowed, scores, 0.0)
        dots = jnp.where(allowed, dots, 0.0)
        part = jnp.sum(scores * dots, axis=0, keepdims=True)
        now = factor[:, start:]
        grad_mix = (now * dots).astype(LOW)
        score_mix = (now * scores).astype(LOW)
        nk_out[local, start : start + rows, :] = nn(grad_mix, query)
        nv_out[local, start : start + rows, :] = nn(score_mix, grad)
        back.append(nn(kt_ref[h, :, start : start + rows], grad_mix))
        weight.append(scale * part)
    return back, weight


def store_sums(ref, h, rows, parts):
    tokens = parts[0].shape[1]
    for i, part in enumerate(parts):
        start = tokens - part.shape[1]
        if i == 0:
            ref[h, rows, :] = part
        else:
            ref[h, rows, start:] += part


def near_kernel(scale, *refs):
    ins, (sum_out, gw_out, nk_out, nv_out) = refs[:6], refs[6:]
    for h in range(sum_out.shape[0]):
        gw_out[h] = jnp.zeros(gw_out.shape[1:], jnp.float32)
        back, weight = near_head(scale, h, *ins, nk_out, nv_out, h)
        store_sums(sum_out, h, slice(None), back)
        store_sums(gw_out, h, pl.ds(0, 1), weight)


def spread(blocks):
    zeros = jnp.zeros_like(blocks[0])
    return jnp.concatenate(
        [
            jnp.concatenate([block if i == j else zeros for j in range(len(blocks))], 1)
            for i, block in enumerate(blocks)
        ],
        0,
    )


def far_kernel(bits, scales, *refs):
    k_ref, v_ref, g_ref, w_ref, qt_ref, _, weight_ref, nk_ref, nv_ref = refs[:9]
    (r1_ref, z2_ref, d2_ref), refs = refs[9:12], refs[12:]
    late_refs, early_refs, refs = refs[: bits - 2], refs[bits - 2 : 2 * bits - 4], refs[2 * bits - 4 :]
    gq_hbm, gk_hbm, gv_hbm, gw_hbm, sum_ref, gq_buf, gk_buf, gv_buf, gw_buf, sems, w_sem = refs
    heads, width, tokens = sum_ref.shape
    half = heads // 2
    place = block_index()
    low_bit = place & 1
    copies = []

    def is_upper(level):
        return ((place >> (level - 1)) & 1) == 1

    def received(level, h):
        if level == 1:
            return r1_ref[h]
        if level == 2:
            return z2_ref[h].astype(jnp.float32) + d2_ref[h].astype(jnp.float32)
        early_ref, late_ref = early_refs[level - 3], late_refs[level - 3]
        early = (low_bit == h // half) == is_upper(level)
        return jnp.where(early, early_ref[h % half], late_ref[h % half])

    def send(i, first, buf, hbm):
        span = pl.ds(first * width, GROUP * width)
        copy = pltpu.make_async_copy(buf.at[first // GROUP], hbm.at[:, span], sems.at[i, first])
        copy.start()
        copies.append(copy)

    gw_buf[...] = weight_ref[...]
    for level in range(1, bits + 1):

        @pl.when(is_upper(level))
        def _():
            for first in range(0, heads, GROUP):
                group = range(first, first + GROUP)
                siblings = spread([received(level, h).astype(LOW) for h in group])
                products = nt(siblings, g_ref[:, first * width : (first + GROUP) * width])
                for i, h in enumerate(group):
                    mine = products[i * width : i * width + width]
                    sum_ref[h] += (scales[level] * w_ref[h, pl.ds(level, 1), :]) * mine
                    gw_buf[h, pl.ds(level, 1), :] = scales[level] * jnp.sum(
                        mine * qt_ref[h].astype(jnp.float32), axis=0, keepdims=True
                    )

    copy = pltpu.make_async_copy(gw_buf, gw_hbm, w_sem)
    copy.start()
    copies.append(copy)
    for first in range(0, heads, GROUP):
        for i in range(GROUP):
            gq_buf[first // GROUP, :, i * width : i * width + width] = sum_ref[first + i].astype(LOW).T
        send(2, first, gq_buf, gq_hbm)
    for first in range(0, heads, GROUP):
        group = range(first, first + GROUP)
        reverses = []
        for h in group:
            total = jnp.zeros((width, width), jnp.float32)
            for level in range(1, bits + 1):
                total = total + jnp.where(is_upper(level), 0, received(level, h)).astype(jnp.float32)
            reverses.append(total.astype(LOW))
        low = spread(reverses)
        near_k = jnp.concatenate([nk_ref[h] for h in group], 1)
        near_v = jnp.concatenate([nv_ref[h] for h in group], 1)
        value = v_ref[:, first * width : (first + GROUP) * width]
        key = k_ref[:, first * width : (first + GROUP) * width]
        gk_buf[first // GROUP] = (near_k + nt(value, low)).astype(LOW)
        gv_buf[first // GROUP] = (near_v + nn(key, low)).astype(LOW)
        send(0, first, gk_buf, gk_hbm)
        send(1, first, gv_buf, gv_hbm)
    for copy in copies:
        copy.wait()


ANY = pl.BlockSpec(memory_space=pl.ANY)
IN_VMEM = pl.BlockSpec(memory_space=pltpu.VMEM)
LIMIT = 16 * 1024 * 1024


def in_hbm(array):
    return pltpu.with_memory_space_constraint(array, pltpu.HBM)


def call(kernel, name, flops, out_shape, operands):
    outs = [pltpu.VMEM(shape, dtype) for shape, dtype in out_shape]
    return pl.pallas_call(
        kernel,
        out_shape=outs,
        in_specs=[IN_VMEM] * len(operands),
        out_specs=[IN_VMEM] * len(outs),
        compiler_params=pltpu.CompilerParams(vmem_limit_bytes=LIMIT),
        cost_estimate=pl.CostEstimate(flops=flops, bytes_accessed=0, transcendentals=0),
        name=name,
    )(*[in_vmem(x) for x in operands])


def on_device(queries, keys, values, out_grad, level_weights):
    tokens = queries.shape[0]
    heads, levels, _ = level_weights.shape
    width = queries.shape[1] // heads
    half = heads // 2
    bits = lax.axis_size(AXES).bit_length() - 1
    scales = level_scales(width, tokens, levels)
    f32 = jnp.float32
    cost = 1000 * tokens * tokens * width
    turned = ((heads, width, tokens), LOW)
    full = ((heads, width, width), LOW)
    halves = (((bits - 2) * half, width, width), LOW)
    weight_rows = ((heads, levels, tokens), f32)
    outs = [turned, halves, halves]
    chosen = pltpu.VMEM((bits - 2, tokens, heads * width), LOW)
    t_v, own, other = pl.pallas_call(
        functools.partial(top_kernel, bits, scales),
        out_shape=[pltpu.VMEM(shape, dtype) for shape, dtype in outs],
        in_specs=[ANY] * 5,
        out_specs=[IN_VMEM] * len(outs),
        scratch_shapes=[
            chosen, chosen, pltpu.VMEM((bits - 2, heads, 1, tokens), f32),
            pltpu.SemaphoreType.DMA((3, bits - 2, CHUNKS)),
        ],
        compiler_params=pltpu.CompilerParams(vmem_limit_bytes=LIMIT),
        cost_estimate=pl.CostEstimate(flops=cost, bytes_accessed=0, transcendentals=0),
        name="top_states",
    )(*[in_hbm(x) for x in (queries, keys, values, out_grad, level_weights)])
    q_v, k_v, v_v, g_v, w_v = queries, keys, values, out_grad, level_weights

    def as_f(array):
        return array.astype(f32)

    got_x = flip(other, 1)
    got_z = flip(own, 2)
    got_d = flip(other, 3)
    quad = as_f(own) + as_f(got_x) + as_f(got_z) + as_f(got_d)
    qt, kt, d2 = call(
        functools.partial(second_kernel, bits, scales[2]), "second_level", cost,
        [turned, turned, full], [q_v, k_v, v_v, g_v, w_v, t_v],
    )
    got_2 = flip(d2, 2)
    (d1,) = call(
        functools.partial(first_kernel, scales[1]), "first_level", cost,
        [full], [v_v, g_v, w_v, qt, kt],
    )
    got_1 = flip(d1, 1)
    sums = []
    for bit in range(2, bits):
        sums.append(quad[:half].astype(LOW))
        quad = quad[half:]
        if bit < bits - 1:
            quad = quad + as_f(flip(quad.astype(LOW), 1 << bit))
    early_half = [swap_halves(x, i + 2, True) for i, x in enumerate(sums)]
    late_half = [swap_halves(x, i + 2, False) for i, x in enumerate(sums)]
    diagonal_2 = flip(got_2, 1)
    total, weights, near_k, near_v = call(
        functools.partial(near_kernel, scales[0]), "near", cost,
        [((heads, width, tokens), f32), weight_rows, *[((heads, tokens, width), f32)] * 2],
        [q_v, k_v, v_v, g_v, w_v, kt],
    )
    operands = [k_v, v_v, g_v, w_v, qt, total, weights, near_k, near_v]
    operands += [got_1, got_2, diagonal_2, *late_half, *early_half]
    out = jax.ShapeDtypeStruct((tokens, heads * width), LOW)
    return pl.pallas_call(
        functools.partial(far_kernel, bits, scales),
        out_shape=(out, out, out, jax.ShapeDtypeStruct((heads, levels, tokens), f32), pltpu.VMEM((heads, width, tokens), f32)),
        in_specs=[IN_VMEM] * len(operands),
        out_specs=(ANY,) * 4 + (IN_VMEM,),
        input_output_aliases={5: 4},
        scratch_shapes=[pltpu.VMEM((heads // GROUP, tokens, GROUP * width), LOW)] * 3
        + [
            pltpu.VMEM((heads, levels, tokens), f32),
            pltpu.SemaphoreType.DMA((3, heads)),
            pltpu.SemaphoreType.DMA,
        ],
        compiler_params=pltpu.CompilerParams(vmem_limit_bytes=LIMIT),
        cost_estimate=pl.CostEstimate(flops=cost, bytes_accessed=0, transcendentals=0),
        name="far",
    )(*[in_vmem(x) for x in operands])[:4]


def solution(mesh):
    rows = P(("groups", "seq", "heads"), "sub")
    weights = P("sub", None, ("groups", "seq", "heads"))
    return jax.shard_map(
        on_device,
        mesh=mesh,
        in_specs=(rows, rows, rows, rows, weights),
        out_specs=(rows, rows, rows, weights),
        check_vma=False,
    )
```

```python
import functools
import math

import jax
import jax.numpy as jnp
from jax import lax
from jax.experimental import pallas as pl
from jax.experimental.pallas import tpu as pltpu
from jax.sharding import PartitionSpec as P

AXES = ("seq", "heads")
LOW = jnp.bfloat16
ROWS = 256
GROUP = 2
CHUNKS = 1


def nt(left, right):
    return lax.dot_general(
        left, right, (((1,), (1,)), ((), ())), preferred_element_type=jnp.float32
    )


def nn(left, right):
    return jnp.dot(left, right, preferred_element_type=jnp.float32)


def flip(block, mask):
    size = lax.axis_size(AXES)
    return lax.ppermute(block, AXES, [(i, i ^ mask) for i in range(size)])


def swap_halves(block, bit, upper_turns):
    routes = []
    for i in range(lax.axis_size(AXES)):
        upper = (i >> bit) & 1 == 1
        routes.append((i, i ^ (1 << bit) ^ (1 if upper == upper_turns else 0)))
    return lax.ppermute(block, AXES, routes)


def block_index():
    return lax.axis_index("seq") * lax.axis_size("heads") + lax.axis_index("heads")


def head(ref, h, width, rows=slice(None)):
    return ref[rows, h * width : (h + 1) * width]


def in_vmem(array):
    return pltpu.with_memory_space_constraint(array, pltpu.VMEM)


def level_scales(width, tokens, count):
    base = 1.0 / math.sqrt(width * tokens)
    return [base] + [base / math.sqrt(2.0 ** (level - 1)) for level in range(1, count)]


def top_kernel(
    bits, scales, q_hbm, k_hbm, v_hbm, g_hbm, w_hbm, t_out, own_out, other_out, left_buf, right_buf, w_buf, sems
):
    heads, width, tokens = t_out.shape
    half = heads // 2
    span = tokens // CHUNKS
    place = block_index()
    low_bit = place & 1

    def copies(index, upper):
        left, right = (q_hbm, g_hbm) if upper else (k_hbm, v_hbm)
        made = []
        for chunk in range(CHUNKS):
            rows = pl.ds(chunk * span, span)
            made.append(
                [
                    pltpu.make_async_copy(left.at[rows], left_buf.at[index, rows], sems.at[0, index, chunk]),
                    pltpu.make_async_copy(right.at[rows], right_buf.at[index, rows], sems.at[1, index, chunk]),
                ]
            )
        if upper:
            level_row = w_hbm.at[:, pl.ds(index + 3, 1), :]
            made[0].append(pltpu.make_async_copy(level_row, w_buf.at[index], sems.at[2, index, 0]))
        return made

    def states(index, upper):
        level = index + 3
        made = copies(index, upper)
        for group in made:
            for copy in group:
                copy.start()
        totals = [None] * (heads // GROUP)
        for chunk, group in enumerate(made):
            for copy in group:
                copy.wait()
            rows = slice(chunk * span, chunk * span + span)
            for pair in range(heads // GROUP):
                lefts = []
                for h in range(pair * GROUP, pair * GROUP + GROUP):
                    turned = left_buf[index, rows, h * width : (h + 1) * width].T
                    if level == bits:
                        t_out[h, :, rows] = turned
                    if upper:
                        turned = (w_buf[index, h, :, rows] * turned.astype(jnp.float32)).astype(LOW)
                    lefts.append(turned)
                columns = slice(pair * GROUP * width, (pair + 1) * GROUP * width)
                part = nn(jnp.concatenate(lefts, 0), right_buf[index, rows, columns])
                totals[pair] = part if totals[pair] is None else totals[pair] + part
        held = []
        for h in range(heads):
            block = slice(h % GROUP * width, h % GROUP * width + width)
            state = totals[h // GROUP][block, block]
            held.append((scales[level] * state if upper else state).astype(LOW))
        for i in range(half):
            low, high = held[i], held[half + i]
            own_out[index * half + i] = jnp.where(low_bit == 0, low, high)
            other_out[index * half + i] = jnp.where(low_bit == 0, high, low)

    for index in range(bits - 2):
        bit = (place >> (index + 2)) & 1
        for value in (0, 1):

            @pl.when(bit == value)
            def _():
                states(index, value == 1)


def mixed_state(level, scale, h, place, query_t, key_t, w_ref, v_ref, g_ref):
    width = query_t.shape[0]
    upper = ((place >> (level - 1)) & 1) == 1
    scaled = (w_ref[h, pl.ds(level, 1), :] * query_t.astype(jnp.float32)).astype(LOW)
    left = jnp.where(upper, scaled, key_t)
    right = jnp.where(upper, head(g_ref, h, width), head(v_ref, h, width))
    return (jnp.where(upper, scale, 1.0) * nn(left, right)).astype(LOW)


def low_kernel(bits, scales, q_ref, k_ref, v_ref, g_ref, w_ref, t_ref, qt_out, kt_out, d1_out, d2_out):
    heads, width = t_ref.shape[:2]
    place = block_index()
    top = ((place >> (bits - 1)) & 1) == 1
    for h in range(heads):
        turned = t_ref[h]
        other = jnp.where(top, head(k_ref, h, width), head(q_ref, h, width)).T
        query_t = jnp.where(top, turned, other)
        key_t = jnp.where(top, other, turned)
        qt_out[h] = query_t
        kt_out[h] = key_t
        for level, out in ((1, d1_out), (2, d2_out)):
            out[h] = mixed_state(
                level, scales[level], h, place, query_t, key_t, w_ref, v_ref, g_ref
            )


def near_head(scale, h, q_ref, k_ref, v_ref, g_ref, w_ref, kt_ref, nk_out, nv_out, local):
    width, tokens = kt_ref.shape[1:]
    rows = min(ROWS, tokens)
    factor = scale * w_ref[h, pl.ds(0, 1), :]
    back, weight = [], []
    for start in range(0, tokens, rows):
        left = tokens - start
        key = head(k_ref, h, width, slice(start, start + rows))
        value = head(v_ref, h, width, slice(start, start + rows))
        query = head(q_ref, h, width, slice(start, None))
        grad = head(g_ref, h, width, slice(start, None))
        scores = nt(key, query)
        dots = nt(value, grad)
        allowed = lax.broadcasted_iota(jnp.int32, (rows, left), 0) <= lax.broadcasted_iota(
            jnp.int32, (rows, left), 1
        )
        scores = jnp.where(allowed, scores, 0.0)
        dots = jnp.where(allowed, dots, 0.0)
        part = jnp.sum(scores * dots, axis=0, keepdims=True)
        now = factor[:, start:]
        grad_mix = (now * dots).astype(LOW)
        score_mix = (now * scores).astype(LOW)
        nk_out[local, start : start + rows, :] = nn(grad_mix, query)
        nv_out[local, start : start + rows, :] = nn(score_mix, grad)
        back.append(nn(kt_ref[h, :, start : start + rows], grad_mix))
        weight.append(scale * part)
    return back, weight


def store_sums(ref, h, rows, parts):
    tokens = parts[0].shape[1]
    for i, part in enumerate(parts):
        start = tokens - part.shape[1]
        if i == 0:
            ref[h, rows, :] = part
        else:
            ref[h, rows, start:] += part


def near_kernel(scale, *refs):
    ins, (sum_out, gw_out, nk_out, nv_out) = refs[:6], refs[6:]
    for h in range(sum_out.shape[0]):
        gw_out[h] = jnp.zeros(gw_out.shape[1:], jnp.float32)
        back, weight = near_head(scale, h, *ins, nk_out, nv_out, h)
        store_sums(sum_out, h, slice(None), back)
        store_sums(gw_out, h, pl.ds(0, 1), weight)


def sum_kernel(*refs):
    *parts, out = refs
    total = parts[0][...].astype(jnp.float32)
    for part in parts[1:]:
        total = total + part[...].astype(jnp.float32)
    out[...] = total.astype(LOW)


def spread(blocks):
    zeros = jnp.zeros_like(blocks[0])
    return jnp.concatenate(
        [
            jnp.concatenate([block if i == j else zeros for j in range(len(blocks))], 1)
            for i, block in enumerate(blocks)
        ],
        0,
    )


def far_kernel(bits, scales, *refs):
    k_ref, v_ref, g_ref, w_ref, qt_ref, _, weight_ref, nk_ref, nv_ref = refs[:9]
    (r1_ref, z2_ref, d2_ref), refs = refs[9:12], refs[12:]
    late_refs, early_refs, refs = refs[: bits - 2], refs[bits - 2 : 2 * bits - 4], refs[2 * bits - 4 :]
    gq_hbm, gk_hbm, gv_hbm, gw_hbm, sum_ref, gq_buf, gk_buf, gv_buf, gw_buf, sems, w_sem = refs
    heads, width, tokens = sum_ref.shape
    half = heads // 2
    place = block_index()
    low_bit = place & 1
    copies = []

    def is_upper(level):
        return ((place >> (level - 1)) & 1) == 1

    def received(level, h):
        if level == 1:
            return r1_ref[h]
        if level == 2:
            return z2_ref[h].astype(jnp.float32) + d2_ref[h].astype(jnp.float32)
        early_ref, late_ref = early_refs[level - 3], late_refs[level - 3]
        early = (low_bit == h // half) == is_upper(level)
        return jnp.where(early, early_ref[h % half], late_ref[h % half])

    def send(i, first, buf, hbm):
        span = pl.ds(first * width, GROUP * width)
        copy = pltpu.make_async_copy(buf.at[first // GROUP], hbm.at[:, span], sems.at[i, first])
        copy.start()
        copies.append(copy)

    gw_buf[...] = weight_ref[...]
    for level in range(1, bits + 1):

        @pl.when(is_upper(level))
        def _():
            for first in range(0, heads, GROUP):
                group = range(first, first + GROUP)
                siblings = spread([received(level, h).astype(LOW) for h in group])
                products = nt(siblings, g_ref[:, first * width : (first + GROUP) * width])
                for i, h in enumerate(group):
                    mine = products[i * width : i * width + width]
                    sum_ref[h] += (scales[level] * w_ref[h, pl.ds(level, 1), :]) * mine
                    gw_buf[h, pl.ds(level, 1), :] = scales[level] * jnp.sum(
                        mine * qt_ref[h].astype(jnp.float32), axis=0, keepdims=True
                    )

    copy = pltpu.make_async_copy(gw_buf, gw_hbm, w_sem)
    copy.start()
    copies.append(copy)
    for first in range(0, heads, GROUP):
        for i in range(GROUP):
            gq_buf[first // GROUP, :, i * width : i * width + width] = sum_ref[first + i].astype(LOW).T
        send(2, first, gq_buf, gq_hbm)
    for first in range(0, heads, GROUP):
        group = range(first, first + GROUP)
        reverses = []
        for h in group:
            total = jnp.zeros((width, width), jnp.float32)
            for level in range(1, bits + 1):
                total = total + jnp.where(is_upper(level), 0, received(level, h)).astype(jnp.float32)
            reverses.append(total.astype(LOW))
        low = spread(reverses)
        near_k = jnp.concatenate([nk_ref[h] for h in group], 1)
        near_v = jnp.concatenate([nv_ref[h] for h in group], 1)
        value = v_ref[:, first * width : (first + GROUP) * width]
        key = k_ref[:, first * width : (first + GROUP) * width]
        gk_buf[first // GROUP] = (near_k + nt(value, low)).astype(LOW)
        gv_buf[first // GROUP] = (near_v + nn(key, low)).astype(LOW)
        send(0, first, gk_buf, gk_hbm)
        send(1, first, gv_buf, gv_hbm)
    for copy in copies:
        copy.wait()


ANY = pl.BlockSpec(memory_space=pl.ANY)
IN_VMEM = pl.BlockSpec(memory_space=pltpu.VMEM)
LIMIT = 16 * 1024 * 1024


def in_hbm(array):
    return pltpu.with_memory_space_constraint(array, pltpu.HBM)


def call(kernel, name, flops, out_shape, operands):
    outs = [pltpu.VMEM(shape, dtype) for shape, dtype in out_shape]
    return pl.pallas_call(
        kernel,
        out_shape=outs,
        in_specs=[IN_VMEM] * len(operands),
        out_specs=[IN_VMEM] * len(outs),
        compiler_params=pltpu.CompilerParams(vmem_limit_bytes=LIMIT),
        cost_estimate=pl.CostEstimate(flops=flops, bytes_accessed=0, transcendentals=0),
        name=name,
    )(*[in_vmem(x) for x in operands])


def on_device(queries, keys, values, out_grad, level_weights):
    tokens = queries.shape[0]
    heads, levels, _ = level_weights.shape
    width = queries.shape[1] // heads
    half = heads // 2
    bits = lax.axis_size(AXES).bit_length() - 1
    scales = level_scales(width, tokens, levels)
    f32 = jnp.float32
    cost = 1000 * tokens * tokens * width
    turned = ((heads, width, tokens), LOW)
    full = ((heads, width, width), LOW)
    halves = (((bits - 2) * half, width, width), LOW)
    weight_rows = ((heads, levels, tokens), f32)
    outs = [turned, halves, halves]
    chosen = pltpu.VMEM((bits - 2, tokens, heads * width), LOW)
    t_v, own, other = pl.pallas_call(
        functools.partial(top_kernel, bits, scales),
        out_shape=[pltpu.VMEM(shape, dtype) for shape, dtype in outs],
        in_specs=[ANY] * 5,
        out_specs=[IN_VMEM] * len(outs),
        scratch_shapes=[
            chosen, chosen, pltpu.VMEM((bits - 2, heads, 1, tokens), f32),
            pltpu.SemaphoreType.DMA((3, bits - 2, CHUNKS)),
        ],
        compiler_params=pltpu.CompilerParams(vmem_limit_bytes=LIMIT),
        cost_estimate=pl.CostEstimate(flops=cost, bytes_accessed=0, transcendentals=0),
        name="top_states",
    )(*[in_hbm(x) for x in (queries, keys, values, out_grad, level_weights)])
    q_v, k_v, v_v, g_v, w_v = queries, keys, values, out_grad, level_weights

    def as_f(array):
        return array.astype(f32)

    got_x = flip(other, 1)
    got_z = flip(own, 2)
    got_d = flip(other, 3)
    (quad,) = call(sum_kernel, "quad_sum", cost, [halves], [own, got_x, got_z, got_d])
    qt, kt, d1, d2 = call(
        functools.partial(low_kernel, bits, scales), "low_states", cost,
        [turned, turned, full, full], [q_v, k_v, v_v, g_v, w_v, t_v],
    )
    got_1 = flip(d1, 1)
    got_2 = flip(d2, 2)
    sums = []
    for bit in range(2, bits):
        sums.append(quad[:half])
        quad = quad[half:]
        if bit < bits - 1:
            quad = (as_f(quad) + as_f(flip(quad, 1 << bit))).astype(LOW)
    early_half = [swap_halves(x, i + 2, True) for i, x in enumerate(sums)]
    late_half = [swap_halves(x, i + 2, False) for i, x in enumerate(sums)]
    diagonal_2 = flip(got_2, 1)
    total, weights, near_k, near_v = call(
        functools.partial(near_kernel, scales[0]), "near", cost,
        [((heads, width, tokens), f32), weight_rows, *[((heads, tokens, width), f32)] * 2],
        [q_v, k_v, v_v, g_v, w_v, kt],
    )
    operands = [k_v, v_v, g_v, w_v, qt, total, weights, near_k, near_v]
    operands += [got_1, got_2, diagonal_2, *late_half, *early_half]
    out = jax.ShapeDtypeStruct((tokens, heads * width), LOW)
    return pl.pallas_call(
        functools.partial(far_kernel, bits, scales),
        out_shape=(out, out, out, jax.ShapeDtypeStruct((heads, levels, tokens), f32), pltpu.VMEM((heads, width, tokens), f32)),
        in_specs=[IN_VMEM] * len(operands),
        out_specs=(ANY,) * 4 + (IN_VMEM,),
        input_output_aliases={5: 4},
        scratch_shapes=[pltpu.VMEM((heads // GROUP, tokens, GROUP * width), LOW)] * 3
        + [
            pltpu.VMEM((heads, levels, tokens), f32),
            pltpu.SemaphoreType.DMA((3, heads)),
            pltpu.SemaphoreType.DMA,
        ],
        compiler_params=pltpu.CompilerParams(vmem_limit_bytes=LIMIT),
        cost_estimate=pl.CostEstimate(flops=cost, bytes_accessed=0, transcendentals=0),
        name="far",
    )(*[in_vmem(x) for x in operands])[:4]


def solution(mesh):
    rows = P(("groups", "seq", "heads"), "sub")
    weights = P("sub", None, ("groups", "seq", "heads"))
    return jax.shard_map(
        on_device,
        mesh=mesh,
        in_specs=(rows, rows, rows, rows, weights),
        out_specs=(rows, rows, rows, weights),
        check_vma=False,
    )
```

```python
import functools
import math

import jax
import jax.numpy as jnp
from jax import lax
from jax.experimental import pallas as pl
from jax.experimental.pallas import tpu as pltpu
from jax.sharding import PartitionSpec as P

AXES = ("seq", "heads")
LOW = jnp.bfloat16
ROWS = 256
GROUP = 2


def nt(left, right):
    return lax.dot_general(
        left, right, (((1,), (1,)), ((), ())), preferred_element_type=jnp.float32
    )


def nn(left, right):
    return jnp.dot(left, right, preferred_element_type=jnp.float32)


def flip(block, mask):
    size = lax.axis_size(AXES)
    return lax.ppermute(block, AXES, [(i, i ^ mask) for i in range(size)])


def swap_halves(block, bit, upper_turns):
    routes = []
    for i in range(lax.axis_size(AXES)):
        upper = (i >> bit) & 1 == 1
        routes.append((i, i ^ (1 << bit) ^ (1 if upper == upper_turns else 0)))
    return lax.ppermute(block, AXES, routes)


def block_index():
    return lax.axis_index("seq") * lax.axis_size("heads") + lax.axis_index("heads")


def head(ref, h, width, rows=slice(None)):
    return ref[rows, h * width : (h + 1) * width]


def in_vmem(array):
    return pltpu.with_memory_space_constraint(array, pltpu.VMEM)


def level_scales(width, tokens, count):
    base = 1.0 / math.sqrt(width * tokens)
    return [base] + [base / math.sqrt(2.0 ** (level - 1)) for level in range(1, count)]


def top_kernel(
    bits, scales, q_hbm, k_hbm, v_hbm, g_hbm, w_hbm, t_out, own_out, other_out, left_buf, right_buf, w_buf, sems
):
    heads, width, tokens = t_out.shape
    half = heads // 2
    place = block_index()
    low_bit = place & 1

    def states(index, upper):
        level = index + 3
        left, right = (q_hbm, g_hbm) if upper else (k_hbm, v_hbm)
        copies = [
            pltpu.make_async_copy(left, left_buf.at[index], sems.at[0, index]),
            pltpu.make_async_copy(right, right_buf.at[index], sems.at[1, index]),
        ]
        if upper:
            level_row = w_hbm.at[:, pl.ds(level, 1), :]
            copies.append(pltpu.make_async_copy(level_row, w_buf.at[index], sems.at[2, index]))
        for copy in copies:
            copy.start()
        for copy in copies:
            copy.wait()
        held = []
        for first in range(0, heads, GROUP):
            lefts = []
            for h in range(first, first + GROUP):
                turned = head(left_buf.at[index], h, width).T
                if level == bits:
                    t_out[h] = turned
                if upper:
                    turned = (w_buf[index, h] * turned.astype(jnp.float32)).astype(LOW)
                lefts.append(turned)
            columns = slice(first * width, (first + GROUP) * width)
            product = nn(jnp.concatenate(lefts, 0), right_buf[index, :, columns])
            for i in range(GROUP):
                block = slice(i * width, i * width + width)
                state = product[block, block]
                held.append((scales[level] * state if upper else state).astype(LOW))
        for i in range(half):
            low, high = held[i], held[half + i]
            own_out[index * half + i] = jnp.where(low_bit == 0, low, high)
            other_out[index * half + i] = jnp.where(low_bit == 0, high, low)

    for index in range(bits - 2):
        bit = (place >> (index + 2)) & 1
        for value in (0, 1):

            @pl.when(bit == value)
            def _():
                states(index, value == 1)


def mixed_state(level, scale, h, place, query_t, key_t, w_ref, v_ref, g_ref):
    width = query_t.shape[0]
    upper = ((place >> (level - 1)) & 1) == 1
    scaled = (w_ref[h, pl.ds(level, 1), :] * query_t.astype(jnp.float32)).astype(LOW)
    left = jnp.where(upper, scaled, key_t)
    right = jnp.where(upper, head(g_ref, h, width), head(v_ref, h, width))
    return (jnp.where(upper, scale, 1.0) * nn(left, right)).astype(LOW)


def low_kernel(bits, scales, q_ref, k_ref, v_ref, g_ref, w_ref, t_ref, qt_out, kt_out, d1_out, d2_out):
    heads, width = t_ref.shape[:2]
    place = block_index()
    top = ((place >> (bits - 1)) & 1) == 1
    for h in range(heads):
        turned = t_ref[h]
        other = jnp.where(top, head(k_ref, h, width), head(q_ref, h, width)).T
        query_t = jnp.where(top, turned, other)
        key_t = jnp.where(top, other, turned)
        qt_out[h] = query_t
        kt_out[h] = key_t
        for level, out in ((1, d1_out), (2, d2_out)):
            out[h] = mixed_state(
                level, scales[level], h, place, query_t, key_t, w_ref, v_ref, g_ref
            )


def near_head(scale, h, q_ref, k_ref, v_ref, g_ref, w_ref, kt_ref, nk_out, nv_out):
    width, tokens = kt_ref.shape[1:]
    rows = min(ROWS, tokens)
    factor = scale * w_ref[h, pl.ds(0, 1), :]
    back, weight = [], []
    for start in range(0, tokens, rows):
        left = tokens - start
        key = head(k_ref, h, width, slice(start, start + rows))
        value = head(v_ref, h, width, slice(start, start + rows))
        query = head(q_ref, h, width, slice(start, None))
        grad = head(g_ref, h, width, slice(start, None))
        scores = nt(key, query)
        dots = nt(value, grad)
        allowed = lax.broadcasted_iota(jnp.int32, (rows, left), 0) <= lax.broadcasted_iota(
            jnp.int32, (rows, left), 1
        )
        scores = jnp.where(allowed, scores, 0.0)
        dots = jnp.where(allowed, dots, 0.0)
        part = jnp.sum(scores * dots, axis=0, keepdims=True)
        now = factor[:, start:]
        grad_mix = (now * dots).astype(LOW)
        score_mix = (now * scores).astype(LOW)
        nk_out[h, start : start + rows, :] = nn(grad_mix, query)
        nv_out[h, start : start + rows, :] = nn(score_mix, grad)
        back.append(nn(kt_ref[h, :, start : start + rows], grad_mix))
        weight.append(scale * part)
    return back, weight


def store_sums(ref, h, rows, parts):
    tokens = parts[0].shape[1]
    for i, part in enumerate(parts):
        start = tokens - part.shape[1]
        if i == 0:
            ref[h, rows, :] = part
        else:
            ref[h, rows, start:] += part


def near_kernel(scale, *refs):
    ins, (sum_out, gw_out, nk_out, nv_out) = refs[:6], refs[6:]
    for h in range(sum_out.shape[0]):
        gw_out[h] = jnp.zeros(gw_out.shape[1:], jnp.float32)
        back, weight = near_head(scale, h, *ins, nk_out, nv_out)
        store_sums(sum_out, h, slice(None), back)
        store_sums(gw_out, h, pl.ds(0, 1), weight)


def copy_kernel(source, out):
    out[...] = source[...]


def sum_kernel(*refs):
    *parts, out = refs
    total = parts[0][...].astype(jnp.float32)
    for part in parts[1:]:
        total = total + part[...].astype(jnp.float32)
    out[...] = total.astype(LOW)


def spread(blocks):
    zeros = jnp.zeros_like(blocks[0])
    return jnp.concatenate(
        [
            jnp.concatenate([block if i == j else zeros for j in range(len(blocks))], 1)
            for i, block in enumerate(blocks)
        ],
        0,
    )


def far_kernel(bits, scales, *refs):
    k_ref, v_ref, g_ref, w_ref, qt_ref, _, weight_ref, nk_ref, nv_ref = refs[:9]
    (r1_ref, z2_ref, d2_ref), refs = refs[9:12], refs[12:]
    late_refs, early_refs, refs = refs[: bits - 2], refs[bits - 2 : 2 * bits - 4], refs[2 * bits - 4 :]
    gq_hbm, gk_hbm, gv_hbm, gw_hbm, sum_ref, gq_buf, gk_buf, gv_buf, gw_buf, sems, w_sem = refs
    heads, width, tokens = sum_ref.shape
    half = heads // 2
    place = block_index()
    low_bit = place & 1
    copies = []

    def is_upper(level):
        return ((place >> (level - 1)) & 1) == 1

    def received(level, h):
        if level == 1:
            return r1_ref[h]
        if level == 2:
            return z2_ref[h].astype(jnp.float32) + d2_ref[h].astype(jnp.float32)
        early_ref, late_ref = early_refs[level - 3], late_refs[level - 3]
        early = (low_bit == h // half) == is_upper(level)
        return jnp.where(early, early_ref[h % half], late_ref[h % half])

    def send(i, first, buf, hbm):
        span = pl.ds(first * width, GROUP * width)
        copy = pltpu.make_async_copy(buf.at[first // GROUP], hbm.at[:, span], sems.at[i, first])
        copy.start()
        copies.append(copy)

    gw_buf[...] = weight_ref[...]
    for level in range(1, bits + 1):

        @pl.when(is_upper(level))
        def _():
            for first in range(0, heads, GROUP):
                group = range(first, first + GROUP)
                siblings = spread([received(level, h).astype(LOW) for h in group])
                products = nt(siblings, g_ref[:, first * width : (first + GROUP) * width])
                for i, h in enumerate(group):
                    mine = products[i * width : i * width + width]
                    sum_ref[h] += (scales[level] * w_ref[h, pl.ds(level, 1), :]) * mine
                    gw_buf[h, pl.ds(level, 1), :] = scales[level] * jnp.sum(
                        mine * qt_ref[h].astype(jnp.float32), axis=0, keepdims=True
                    )

    copy = pltpu.make_async_copy(gw_buf, gw_hbm, w_sem)
    copy.start()
    copies.append(copy)
    for first in range(0, heads, GROUP):
        for i in range(GROUP):
            gq_buf[first // GROUP, :, i * width : i * width + width] = sum_ref[first + i].astype(LOW).T
        send(2, first, gq_buf, gq_hbm)
    for first in range(0, heads, GROUP):
        group = range(first, first + GROUP)
        reverses = []
        for h in group:
            total = jnp.zeros((width, width), jnp.float32)
            for level in range(1, bits + 1):
                total = total + jnp.where(is_upper(level), 0, received(level, h)).astype(jnp.float32)
            reverses.append(total.astype(LOW))
        low = spread(reverses)
        near_k = jnp.concatenate([nk_ref[h] for h in group], 1)
        near_v = jnp.concatenate([nv_ref[h] for h in group], 1)
        value = v_ref[:, first * width : (first + GROUP) * width]
        key = k_ref[:, first * width : (first + GROUP) * width]
        gk_buf[first // GROUP] = (near_k + nt(value, low)).astype(LOW)
        gv_buf[first // GROUP] = (near_v + nn(key, low)).astype(LOW)
        send(0, first, gk_buf, gk_hbm)
        send(1, first, gv_buf, gv_hbm)
    for copy in copies:
        copy.wait()


ANY = pl.BlockSpec(memory_space=pl.ANY)
IN_VMEM = pl.BlockSpec(memory_space=pltpu.VMEM)
LIMIT = 16 * 1024 * 1024


def in_hbm(array):
    return pltpu.with_memory_space_constraint(array, pltpu.HBM)


def call(kernel, name, flops, out_shape, operands):
    outs = [pltpu.VMEM(shape, dtype) for shape, dtype in out_shape]
    return pl.pallas_call(
        kernel,
        out_shape=outs,
        in_specs=[IN_VMEM] * len(operands),
        out_specs=[IN_VMEM] * len(outs),
        compiler_params=pltpu.CompilerParams(vmem_limit_bytes=LIMIT),
        cost_estimate=pl.CostEstimate(flops=flops, bytes_accessed=0, transcendentals=0),
        name=name,
    )(*[in_vmem(x) for x in operands])


def on_device(queries, keys, values, out_grad, level_weights):
    tokens = queries.shape[0]
    heads, levels, _ = level_weights.shape
    width = queries.shape[1] // heads
    half = heads // 2
    bits = lax.axis_size(AXES).bit_length() - 1
    scales = level_scales(width, tokens, levels)
    f32 = jnp.float32
    cost = 1000 * tokens * tokens * width
    turned = ((heads, width, tokens), LOW)
    full = ((heads, width, width), LOW)
    halves = (((bits - 2) * half, width, width), LOW)
    weight_rows = ((heads, levels, tokens), f32)
    outs = [turned, halves, halves]
    chosen = pltpu.VMEM((bits - 2, tokens, heads * width), LOW)
    t_v, own, other = pl.pallas_call(
        functools.partial(top_kernel, bits, scales),
        out_shape=[pltpu.VMEM(shape, dtype) for shape, dtype in outs],
        in_specs=[ANY] * 5,
        out_specs=[IN_VMEM] * len(outs),
        scratch_shapes=[
            chosen, chosen, pltpu.VMEM((bits - 2, heads, 1, tokens), f32),
            pltpu.SemaphoreType.DMA((3, bits - 2)),
        ],
        compiler_params=pltpu.CompilerParams(vmem_limit_bytes=LIMIT),
        cost_estimate=pl.CostEstimate(flops=cost, bytes_accessed=0, transcendentals=0),
        name="top_states",
    )(*[in_hbm(x) for x in (queries, keys, values, out_grad, level_weights)])

    def as_f(array):
        return array.astype(f32)

    got_z = flip(own, 2)
    got_d = flip(other, 3)
    (other_x,) = call(copy_kernel, "x_part", cost, [halves], [other])
    got_x = flip(other_x, 1)
    (quad,) = call(sum_kernel, "quad_sum", cost, [halves], [own, got_x, got_z, got_d])
    qt, kt, d1, d2 = call(
        functools.partial(low_kernel, bits, scales), "low_states", cost,
        [turned, turned, full, full], [queries, keys, values, out_grad, level_weights, t_v],
    )
    got_1 = flip(d1, 1)
    got_2 = flip(d2, 2)
    sums = []
    for bit in range(2, bits):
        sums.append(quad[:half])
        quad = quad[half:]
        if bit < bits - 1:
            quad = (as_f(quad) + as_f(flip(quad, 1 << bit))).astype(LOW)
    early_half = [swap_halves(x, i + 2, True) for i, x in enumerate(sums)]
    late_half = [swap_halves(x, i + 2, False) for i, x in enumerate(sums)]
    diagonal_2 = flip(got_2, 1)
    total, weights, near_k, near_v = call(
        functools.partial(near_kernel, scales[0]), "near", cost,
        [((heads, width, tokens), f32), weight_rows, *[((heads, tokens, width), f32)] * 2],
        [queries, keys, values, out_grad, level_weights, kt],
    )
    operands = [keys, values, out_grad, level_weights, qt, total, weights, near_k, near_v]
    operands += [got_1, got_2, diagonal_2, *late_half, *early_half]
    out = jax.ShapeDtypeStruct((tokens, heads * width), LOW)
    return pl.pallas_call(
        functools.partial(far_kernel, bits, scales),
        out_shape=(
            out, out, out, jax.ShapeDtypeStruct((heads, levels, tokens), f32),
            pltpu.VMEM((heads, width, tokens), f32),
        ),
        in_specs=[IN_VMEM] * len(operands),
        out_specs=(ANY,) * 4 + (IN_VMEM,),
        input_output_aliases={5: 4},
        scratch_shapes=[pltpu.VMEM((heads // GROUP, tokens, GROUP * width), LOW)] * 3
        + [
            pltpu.VMEM((heads, levels, tokens), f32),
            pltpu.SemaphoreType.DMA((3, heads)),
            pltpu.SemaphoreType.DMA,
        ],
        compiler_params=pltpu.CompilerParams(vmem_limit_bytes=LIMIT),
        cost_estimate=pl.CostEstimate(flops=cost, bytes_accessed=0, transcendentals=0),
        name="far",
    )(*[in_vmem(x) for x in operands])[:4]


def solution(mesh):
    rows = P(("groups", "seq", "heads"), "sub")
    weights = P("sub", None, ("groups", "seq", "heads"))
    return jax.shard_map(
        on_device,
        mesh=mesh,
        in_specs=(rows, rows, rows, rows, weights),
        out_specs=(rows, rows, rows, weights),
        check_vma=False,
    )
```

```python
import functools
import math

import jax
import jax.numpy as jnp
from jax import lax
from jax.experimental import pallas as pl
from jax.experimental.pallas import tpu as pltpu
from jax.sharding import PartitionSpec as P

AXES = ("seq", "heads")
LOW = jnp.bfloat16
ROWS = 256
GROUP = 2


def nt(left, right):
    return lax.dot_general(
        left, right, (((1,), (1,)), ((), ())), preferred_element_type=jnp.float32
    )


def nn(left, right):
    return jnp.dot(left, right, preferred_element_type=jnp.float32)


def flip(block, mask):
    size = lax.axis_size(AXES)
    return lax.ppermute(block, AXES, [(i, i ^ mask) for i in range(size)])


def swap_halves(block, bit, upper_turns):
    routes = []
    for i in range(lax.axis_size(AXES)):
        upper = (i >> bit) & 1 == 1
        routes.append((i, i ^ (1 << bit) ^ (1 if upper == upper_turns else 0)))
    return lax.ppermute(block, AXES, routes)


def block_index():
    return lax.axis_index("seq") * lax.axis_size("heads") + lax.axis_index("heads")


def head(ref, h, width, rows=slice(None)):
    return ref[rows, h * width : (h + 1) * width]


def in_vmem(array):
    return pltpu.with_memory_space_constraint(array, pltpu.VMEM)


def level_scales(width, tokens, count):
    base = 1.0 / math.sqrt(width * tokens)
    return [base] + [base / math.sqrt(2.0 ** (level - 1)) for level in range(1, count)]


def top_kernel(
    bits, scales, q_hbm, k_hbm, v_hbm, g_hbm, w_hbm, t_out, own_out, other_out, left_buf, right_buf, w_buf, sems
):
    heads, width, tokens = t_out.shape
    half = heads // 2
    place = block_index()
    low_bit = place & 1

    def states(index, upper):
        level = index + 3
        left, right = (q_hbm, g_hbm) if upper else (k_hbm, v_hbm)
        copies = [
            pltpu.make_async_copy(left, left_buf.at[index], sems.at[0, index]),
            pltpu.make_async_copy(right, right_buf.at[index], sems.at[1, index]),
        ]
        if upper:
            level_row = w_hbm.at[:, pl.ds(level, 1), :]
            copies.append(pltpu.make_async_copy(level_row, w_buf.at[index], sems.at[2, index]))
        for copy in copies:
            copy.start()
        for copy in copies:
            copy.wait()
        held = []
        for first in range(0, heads, GROUP):
            lefts = []
            for h in range(first, first + GROUP):
                turned = head(left_buf.at[index], h, width).T
                if level == bits:
                    t_out[h] = turned
                if upper:
                    turned = (w_buf[index, h] * turned.astype(jnp.float32)).astype(LOW)
                lefts.append(turned)
            columns = slice(first * width, (first + GROUP) * width)
            product = nn(jnp.concatenate(lefts, 0), right_buf[index, :, columns])
            for i in range(GROUP):
                block = slice(i * width, i * width + width)
                state = product[block, block]
                held.append((scales[level] * state if upper else state).astype(LOW))
        for i in range(half):
            low, high = held[i], held[half + i]
            own_out[index * half + i] = jnp.where(low_bit == 0, low, high)
            other_out[index * half + i] = jnp.where(low_bit == 0, high, low)

    for index in range(bits - 2):
        bit = (place >> (index + 2)) & 1
        for value in (0, 1):

            @pl.when(bit == value)
            def _():
                states(index, value == 1)


def mixed_state(level, scale, h, place, query_t, key_t, w_ref, v_ref, g_ref):
    width = query_t.shape[0]
    upper = ((place >> (level - 1)) & 1) == 1
    scaled = (w_ref[h, pl.ds(level, 1), :] * query_t.astype(jnp.float32)).astype(LOW)
    left = jnp.where(upper, scaled, key_t)
    right = jnp.where(upper, head(g_ref, h, width), head(v_ref, h, width))
    return (jnp.where(upper, scale, 1.0) * nn(left, right)).astype(LOW)


def low_kernel(bits, scales, q_ref, k_ref, v_ref, g_ref, w_ref, t_ref, qt_out, kt_out, d1_out, d2_out):
    heads, width = t_ref.shape[:2]
    place = block_index()
    top = ((place >> (bits - 1)) & 1) == 1
    for h in range(heads):
        turned = t_ref[h]
        other = jnp.where(top, head(k_ref, h, width), head(q_ref, h, width)).T
        query_t = jnp.where(top, turned, other)
        key_t = jnp.where(top, other, turned)
        qt_out[h] = query_t
        kt_out[h] = key_t
        for level, out in ((1, d1_out), (2, d2_out)):
            out[h] = mixed_state(
                level, scales[level], h, place, query_t, key_t, w_ref, v_ref, g_ref
            )


def near_head(scale, h, q_ref, k_ref, v_ref, g_ref, w_ref, kt_ref, nk_out, nv_out):
    width, tokens = kt_ref.shape[1:]
    rows = min(ROWS, tokens)
    factor = scale * w_ref[h, pl.ds(0, 1), :]
    back, weight = [], []
    for start in range(0, tokens, rows):
        left = tokens - start
        key = head(k_ref, h, width, slice(start, start + rows))
        value = head(v_ref, h, width, slice(start, start + rows))
        query = head(q_ref, h, width, slice(start, None))
        grad = head(g_ref, h, width, slice(start, None))
        scores = nt(key, query)
        dots = nt(value, grad)
        allowed = lax.broadcasted_iota(jnp.int32, (rows, left), 0) <= lax.broadcasted_iota(
            jnp.int32, (rows, left), 1
        )
        scores = jnp.where(allowed, scores, 0.0)
        dots = jnp.where(allowed, dots, 0.0)
        part = jnp.sum(scores * dots, axis=0, keepdims=True)
        now = factor[:, start:]
        grad_mix = (now * dots).astype(LOW)
        score_mix = (now * scores).astype(LOW)
        nk_out[h, start : start + rows, :] = nn(grad_mix, query)
        nv_out[h, start : start + rows, :] = nn(score_mix, grad)
        back.append(nn(kt_ref[h, :, start : start + rows], grad_mix))
        weight.append(scale * part)
    return back, weight


def store_sums(ref, h, rows, parts):
    tokens = parts[0].shape[1]
    for i, part in enumerate(parts):
        start = tokens - part.shape[1]
        if i == 0:
            ref[h, rows, :] = part
        else:
            ref[h, rows, start:] += part


def near_kernel(scale, *refs):
    ins, (sum_out, gw_out, nk_out, nv_out, gq_out) = refs[:6], refs[6:]
    for h in range(sum_out.shape[0]):
        gw_out[h] = jnp.zeros(gw_out.shape[1:], jnp.float32)
        back, weight = near_head(scale, h, *ins, nk_out, nv_out)
        store_sums(sum_out, h, slice(None), back)
        store_sums(gw_out, h, pl.ds(0, 1), weight)

    @pl.when(block_index() == 0)
    def _():
        store_queries(sum_out, gq_out)


def store_queries(sum_ref, gq_ref):
    heads, width, _ = sum_ref.shape
    for h in range(heads):
        gq_ref[:, h * width : (h + 1) * width] = sum_ref[h].astype(LOW).T


def copy_kernel(source, out):
    out[...] = source[...]


def sum_kernel(*refs):
    *parts, out = refs
    total = parts[0][...].astype(jnp.float32)
    for part in parts[1:]:
        total = total + part[...].astype(jnp.float32)
    out[...] = total.astype(LOW)


def spread(blocks):
    zeros = jnp.zeros_like(blocks[0])
    return jnp.concatenate(
        [
            jnp.concatenate([block if i == j else zeros for j in range(len(blocks))], 1)
            for i, block in enumerate(blocks)
        ],
        0,
    )


def far_kernel(bits, scales, *refs):
    k_ref, v_ref, g_ref, w_ref, qt_ref, _, weight_ref, nk_ref, nv_ref = refs[:9]
    (gq_ref, r1_ref, z2_ref, d2_ref), refs = refs[9:13], refs[13:]
    late_refs, early_refs, refs = refs[: bits - 2], refs[bits - 2 : 2 * bits - 4], refs[2 * bits - 4 :]
    gq_hbm, gk_hbm, gv_hbm, gw_hbm, sum_ref, gq_buf, gk_buf, gv_buf, gw_buf, sems, w_sem, gq_sem = refs
    heads, width, tokens = sum_ref.shape
    half = heads // 2
    place = block_index()
    low_bit = place & 1
    copies = []

    def is_upper(level):
        return ((place >> (level - 1)) & 1) == 1

    def received(level, h):
        if level == 1:
            return r1_ref[h]
        if level == 2:
            return z2_ref[h].astype(jnp.float32) + d2_ref[h].astype(jnp.float32)
        early_ref, late_ref = early_refs[level - 3], late_refs[level - 3]
        early = (low_bit == h // half) == is_upper(level)
        return jnp.where(early, early_ref[h % half], late_ref[h % half])

    def send(i, first, buf, hbm):
        span = pl.ds(first * width, GROUP * width)
        copy = pltpu.make_async_copy(buf.at[first // GROUP], hbm.at[:, span], sems.at[i, first])
        copy.start()
        copies.append(copy)

    @pl.when(place == 0)
    def _():
        pltpu.make_async_copy(gq_ref, gq_hbm, gq_sem).start()

    gw_buf[...] = weight_ref[...]
    for level in range(1, bits + 1):

        @pl.when(is_upper(level))
        def _():
            for first in range(0, heads, GROUP):
                group = range(first, first + GROUP)
                siblings = spread([received(level, h).astype(LOW) for h in group])
                products = nt(siblings, g_ref[:, first * width : (first + GROUP) * width])
                for i, h in enumerate(group):
                    mine = products[i * width : i * width + width]
                    sum_ref[h] += (scales[level] * w_ref[h, pl.ds(level, 1), :]) * mine
                    gw_buf[h, pl.ds(level, 1), :] = scales[level] * jnp.sum(
                        mine * qt_ref[h].astype(jnp.float32), axis=0, keepdims=True
                    )

    copy = pltpu.make_async_copy(gw_buf, gw_hbm, w_sem)
    copy.start()
    copies.append(copy)

    @pl.when(place != 0)
    def _():
        store_queries(sum_ref, gq_buf)
        pltpu.make_async_copy(gq_buf, gq_hbm, gq_sem).start()

    for first in range(0, heads, GROUP):
        group = range(first, first + GROUP)
        reverses = []
        for h in group:
            total = jnp.zeros((width, width), jnp.float32)
            for level in range(1, bits + 1):
                total = total + jnp.where(is_upper(level), 0, received(level, h)).astype(jnp.float32)
            reverses.append(total.astype(LOW))
        low = spread(reverses)
        near_k = jnp.concatenate([nk_ref[h] for h in group], 1)
        near_v = jnp.concatenate([nv_ref[h] for h in group], 1)
        value = v_ref[:, first * width : (first + GROUP) * width]
        key = k_ref[:, first * width : (first + GROUP) * width]
        gk_buf[first // GROUP] = (near_k + nt(value, low)).astype(LOW)
        gv_buf[first // GROUP] = (near_v + nn(key, low)).astype(LOW)
        send(0, first, gk_buf, gk_hbm)
        send(1, first, gv_buf, gv_hbm)
    pltpu.make_async_copy(gq_buf, gq_hbm, gq_sem).wait()
    for copy in copies:
        copy.wait()


ANY = pl.BlockSpec(memory_space=pl.ANY)
IN_VMEM = pl.BlockSpec(memory_space=pltpu.VMEM)
LIMIT = 16 * 1024 * 1024


def in_hbm(array):
    return pltpu.with_memory_space_constraint(array, pltpu.HBM)


def call(kernel, name, flops, out_shape, operands):
    outs = [pltpu.VMEM(shape, dtype) for shape, dtype in out_shape]
    return pl.pallas_call(
        kernel,
        out_shape=outs,
        in_specs=[IN_VMEM] * len(operands),
        out_specs=[IN_VMEM] * len(outs),
        compiler_params=pltpu.CompilerParams(vmem_limit_bytes=LIMIT),
        cost_estimate=pl.CostEstimate(flops=flops, bytes_accessed=0, transcendentals=0),
        name=name,
    )(*[in_vmem(x) for x in operands])


def on_device(queries, keys, values, out_grad, level_weights):
    tokens = queries.shape[0]
    heads, levels, _ = level_weights.shape
    width = queries.shape[1] // heads
    half = heads // 2
    bits = lax.axis_size(AXES).bit_length() - 1
    scales = level_scales(width, tokens, levels)
    f32 = jnp.float32
    cost = 1000 * tokens * tokens * width
    turned = ((heads, width, tokens), LOW)
    full = ((heads, width, width), LOW)
    halves = (((bits - 2) * half, width, width), LOW)
    weight_rows = ((heads, levels, tokens), f32)
    outs = [turned, halves, halves]
    chosen = pltpu.VMEM((bits - 2, tokens, heads * width), LOW)
    t_v, own, other = pl.pallas_call(
        functools.partial(top_kernel, bits, scales),
        out_shape=[pltpu.VMEM(shape, dtype) for shape, dtype in outs],
        in_specs=[ANY] * 5,
        out_specs=[IN_VMEM] * len(outs),
        scratch_shapes=[
            chosen, chosen, pltpu.VMEM((bits - 2, heads, 1, tokens), f32),
            pltpu.SemaphoreType.DMA((3, bits - 2)),
        ],
        compiler_params=pltpu.CompilerParams(vmem_limit_bytes=LIMIT),
        cost_estimate=pl.CostEstimate(flops=cost, bytes_accessed=0, transcendentals=0),
        name="top_states",
    )(*[in_hbm(x) for x in (queries, keys, values, out_grad, level_weights)])

    def as_f(array):
        return array.astype(f32)

    got_z = flip(own, 2)
    got_d = flip(other, 3)
    (other_x,) = call(copy_kernel, "x_part", cost, [halves], [other])
    got_x = flip(other_x, 1)
    (quad,) = call(sum_kernel, "quad_sum", cost, [halves], [own, got_x, got_z, got_d])
    qt, kt, d1, d2 = call(
        functools.partial(low_kernel, bits, scales), "low_states", cost,
        [turned, turned, full, full], [queries, keys, values, out_grad, level_weights, t_v],
    )
    got_1 = flip(d1, 1)
    got_2 = flip(d2, 2)
    sums = []
    for bit in range(2, bits):
        sums.append(quad[:half])
        quad = quad[half:]
        if bit < bits - 1:
            quad = (as_f(quad) + as_f(flip(quad, 1 << bit))).astype(LOW)
    early_half = [swap_halves(x, i + 2, True) for i, x in enumerate(sums)]
    late_half = [swap_halves(x, i + 2, False) for i, x in enumerate(sums)]
    diagonal_2 = flip(got_2, 1)
    flat = ((tokens, heads * width), LOW)
    total, weights, near_k, near_v, early_q = call(
        functools.partial(near_kernel, scales[0]), "near", cost,
        [((heads, width, tokens), f32), weight_rows, *[((heads, tokens, width), f32)] * 2, flat],
        [queries, keys, values, out_grad, level_weights, kt],
    )
    operands = [keys, values, out_grad, level_weights, qt, total, weights, near_k, near_v]
    operands += [early_q, got_1, got_2, diagonal_2, *late_half, *early_half]
    out = jax.ShapeDtypeStruct((tokens, heads * width), LOW)
    return pl.pallas_call(
        functools.partial(far_kernel, bits, scales),
        out_shape=(
            out, out, out, jax.ShapeDtypeStruct((heads, levels, tokens), f32),
            pltpu.VMEM((heads, width, tokens), f32),
        ),
        in_specs=[IN_VMEM] * len(operands),
        out_specs=(ANY,) * 4 + (IN_VMEM,),
        input_output_aliases={5: 4},
        scratch_shapes=[pltpu.VMEM(*flat)]
        + [pltpu.VMEM((heads // GROUP, tokens, GROUP * width), LOW)] * 2
        + [
            pltpu.VMEM((heads, levels, tokens), f32),
            pltpu.SemaphoreType.DMA((2, heads)),
            pltpu.SemaphoreType.DMA,
            pltpu.SemaphoreType.DMA,
        ],
        compiler_params=pltpu.CompilerParams(vmem_limit_bytes=LIMIT),
        cost_estimate=pl.CostEstimate(flops=cost, bytes_accessed=0, transcendentals=0),
        name="far",
    )(*[in_vmem(x) for x in operands])[:4]


def solution(mesh):
    rows = P(("groups", "seq", "heads"), "sub")
    weights = P("sub", None, ("groups", "seq", "heads"))
    return jax.shard_map(
        on_device,
        mesh=mesh,
        in_specs=(rows, rows, rows, rows, weights),
        out_specs=(rows, rows, rows, weights),
        check_vma=False,
    )
```

```python
import functools
import math

import jax
import jax.numpy as jnp
from jax import lax
from jax.experimental import pallas as pl
from jax.experimental.pallas import tpu as pltpu
from jax.sharding import PartitionSpec as P

AXES = ("seq", "heads")
LOW = jnp.bfloat16
ROWS = 256
GROUP = 2


def nt(left, right):
    return lax.dot_general(
        left, right, (((1,), (1,)), ((), ())), preferred_element_type=jnp.float32
    )


def nn(left, right):
    return jnp.dot(left, right, preferred_element_type=jnp.float32)


def flip(block, mask):
    size = lax.axis_size(AXES)
    return lax.ppermute(block, AXES, [(i, i ^ mask) for i in range(size)])


def swap_halves(block, bit, upper_turns):
    routes = []
    for i in range(lax.axis_size(AXES)):
        upper = (i >> bit) & 1 == 1
        routes.append((i, i ^ (1 << bit) ^ (1 if upper == upper_turns else 0)))
    return lax.ppermute(block, AXES, routes)


def block_index():
    return lax.axis_index("seq") * lax.axis_size("heads") + lax.axis_index("heads")


def head(ref, h, width, rows=slice(None)):
    return ref[rows, h * width : (h + 1) * width]


def in_vmem(array):
    return pltpu.with_memory_space_constraint(array, pltpu.VMEM)


def level_scales(width, tokens, count):
    base = 1.0 / math.sqrt(width * tokens)
    return [base] + [base / math.sqrt(2.0 ** (level - 1)) for level in range(1, count)]


def top_kernel(
    bits, scales, q_hbm, k_hbm, v_hbm, g_hbm, w_hbm, t_out, own_out, other_out, left_buf, right_buf, w_buf, sems
):
    heads, width, tokens = t_out.shape
    half = heads // 2
    place = block_index()
    low_bit = place & 1

    def states(index, upper):
        level = index + 3
        left, right = (q_hbm, g_hbm) if upper else (k_hbm, v_hbm)
        copies = [
            pltpu.make_async_copy(left, left_buf.at[index], sems.at[0, index]),
            pltpu.make_async_copy(right, right_buf.at[index], sems.at[1, index]),
        ]
        if upper:
            level_row = w_hbm.at[:, pl.ds(level, 1), :]
            copies.append(pltpu.make_async_copy(level_row, w_buf.at[index], sems.at[2, index]))
        for copy in copies:
            copy.start()
        for copy in copies:
            copy.wait()
        held = []
        for first in range(0, heads, GROUP):
            lefts = []
            for h in range(first, first + GROUP):
                turned = head(left_buf.at[index], h, width).T
                if level == bits:
                    t_out[h] = turned
                if upper:
                    turned = (w_buf[index, h] * turned.astype(jnp.float32)).astype(LOW)
                lefts.append(turned)
            columns = slice(first * width, (first + GROUP) * width)
            product = nn(jnp.concatenate(lefts, 0), right_buf[index, :, columns])
            for i in range(GROUP):
                block = slice(i * width, i * width + width)
                state = product[block, block]
                held.append((scales[level] * state if upper else state).astype(LOW))
        for i in range(half):
            low, high = held[i], held[half + i]
            own_out[index * half + i] = jnp.where(low_bit == 0, low, high)
            other_out[index * half + i] = jnp.where(low_bit == 0, high, low)

    for index in range(bits - 2):
        bit = (place >> (index + 2)) & 1
        for value in (0, 1):

            @pl.when(bit == value)
            def _():
                states(index, value == 1)


def mixed_state(level, scale, h, place, query_t, key_t, w_ref, v_ref, g_ref):
    width = query_t.shape[0]
    upper = ((place >> (level - 1)) & 1) == 1
    scaled = (w_ref[h, pl.ds(level, 1), :] * query_t.astype(jnp.float32)).astype(LOW)
    left = jnp.where(upper, scaled, key_t)
    right = jnp.where(upper, head(g_ref, h, width), head(v_ref, h, width))
    return (jnp.where(upper, scale, 1.0) * nn(left, right)).astype(LOW)


def low_kernel(bits, scales, q_ref, k_ref, v_ref, g_ref, w_ref, t_ref, qt_out, kt_out, d1_out, d2_out):
    heads, width = t_ref.shape[:2]
    place = block_index()
    top = ((place >> (bits - 1)) & 1) == 1
    for h in range(heads):
        turned = t_ref[h]
        other = jnp.where(top, head(k_ref, h, width), head(q_ref, h, width)).T
        query_t = jnp.where(top, turned, other)
        key_t = jnp.where(top, other, turned)
        qt_out[h] = query_t
        kt_out[h] = key_t
        for level, out in ((1, d1_out), (2, d2_out)):
            out[h] = mixed_state(
                level, scales[level], h, place, query_t, key_t, w_ref, v_ref, g_ref
            )


def near_head(scale, h, q_ref, k_ref, v_ref, g_ref, w_ref, kt_ref, nk_out, nv_out):
    width, tokens = kt_ref.shape[1:]
    rows = min(ROWS, tokens)
    factor = scale * w_ref[h, pl.ds(0, 1), :]
    back, weight = [], []
    for start in range(0, tokens, rows):
        left = tokens - start
        key = head(k_ref, h, width, slice(start, start + rows))
        value = head(v_ref, h, width, slice(start, start + rows))
        query = head(q_ref, h, width, slice(start, None))
        grad = head(g_ref, h, width, slice(start, None))
        scores = nt(key, query)
        dots = nt(value, grad)
        allowed = lax.broadcasted_iota(jnp.int32, (rows, left), 0) <= lax.broadcasted_iota(
            jnp.int32, (rows, left), 1
        )
        scores = jnp.where(allowed, scores, 0.0)
        dots = jnp.where(allowed, dots, 0.0)
        part = jnp.sum(scores * dots, axis=0, keepdims=True)
        now = factor[:, start:]
        grad_mix = (now * dots).astype(LOW)
        score_mix = (now * scores).astype(LOW)
        nk_out[h, start : start + rows, :] = nn(grad_mix, query)
        nv_out[h, start : start + rows, :] = nn(score_mix, grad)
        back.append(nn(kt_ref[h, :, start : start + rows], grad_mix))
        weight.append(scale * part)
    return back, weight


def store_sums(ref, h, rows, parts):
    tokens = parts[0].shape[1]
    for i, part in enumerate(parts):
        start = tokens - part.shape[1]
        if i == 0:
            ref[h, rows, :] = part
        else:
            ref[h, rows, start:] += part


def near_kernel(scale, *refs):
    ins, (sum_out, gw_out, nk_out, nv_out, gq_out) = refs[:6], refs[6:]
    for h in range(sum_out.shape[0]):
        gw_out[h] = jnp.zeros(gw_out.shape[1:], jnp.float32)
        back, weight = near_head(scale, h, *ins, nk_out, nv_out)
        store_sums(sum_out, h, slice(None), back)
        store_sums(gw_out, h, pl.ds(0, 1), weight)

    @pl.when(block_index() == 0)
    def _():
        store_queries(sum_out, gq_out)


def store_queries(sum_ref, gq_ref):
    heads, width, _ = sum_ref.shape
    for h in range(heads):
        gq_ref[:, h * width : (h + 1) * width] = sum_ref[h].astype(LOW).T


def copy_kernel(source, out):
    out[...] = source[...]


def sum_kernel(*refs):
    *parts, out = refs
    total = parts[0][...].astype(jnp.float32)
    for part in parts[1:]:
        total = total + part[...].astype(jnp.float32)
    out[...] = total.astype(LOW)


def spread(blocks):
    zeros = jnp.zeros_like(blocks[0])
    return jnp.concatenate(
        [
            jnp.concatenate([block if i == j else zeros for j in range(len(blocks))], 1)
            for i, block in enumerate(blocks)
        ],
        0,
    )


def far_kernel(bits, scales, *refs):
    k_ref, v_ref, g_ref, w_ref, qt_ref, _, weight_ref, nk_ref, nv_ref = refs[:9]
    (gq_ref, r1_ref, z2_ref, d2_ref), refs = refs[9:13], refs[13:]
    late_refs, early_refs, refs = refs[: bits - 2], refs[bits - 2 : 2 * bits - 4], refs[2 * bits - 4 :]
    gq_hbm, gk_hbm, gv_hbm, gw_hbm, sum_ref, gq_buf, gk_buf, gv_buf, gw_buf, sems, w_sem, gq_sem = refs
    heads, width, tokens = sum_ref.shape
    half = heads // 2
    place = block_index()
    low_bit = place & 1
    copies = []

    def is_upper(level):
        return ((place >> (level - 1)) & 1) == 1

    def received(level, h):
        if level == 1:
            return r1_ref[h]
        if level == 2:
            return z2_ref[h].astype(jnp.float32) + d2_ref[h].astype(jnp.float32)
        early_ref, late_ref = early_refs[level - 3], late_refs[level - 3]
        early = (low_bit == h // half) == is_upper(level)
        return jnp.where(early, early_ref[h % half], late_ref[h % half])

    def send(i, first, buf, hbm):
        span = pl.ds(first * width, GROUP * width)
        copy = pltpu.make_async_copy(buf.at[first // GROUP], hbm.at[:, span], sems.at[i, first])
        copy.start()
        copies.append(copy)

    @pl.when(place == 0)
    def _():
        pltpu.make_async_copy(gq_ref, gq_hbm, gq_sem).start()

    gw_buf[...] = weight_ref[...]
    for level in range(1, bits + 1):

        @pl.when(is_upper(level))
        def _():
            for first in range(0, heads, GROUP):
                group = range(first, first + GROUP)
                siblings = spread([received(level, h).astype(LOW) for h in group])
                products = nt(siblings, g_ref[:, first * width : (first + GROUP) * width])
                for i, h in enumerate(group):
                    mine = products[i * width : i * width + width]
                    sum_ref[h] += (scales[level] * w_ref[h, pl.ds(level, 1), :]) * mine
                    gw_buf[h, pl.ds(level, 1), :] = scales[level] * jnp.sum(
                        mine * qt_ref[h].astype(jnp.float32), axis=0, keepdims=True
                    )

    copy = pltpu.make_async_copy(gw_buf, gw_hbm, w_sem)
    copy.start()
    copies.append(copy)

    @pl.when(place != 0)
    def _():
        store_queries(sum_ref, gq_buf)
        pltpu.make_async_copy(gq_buf, gq_hbm, gq_sem).start()

    for first in range(0, heads, GROUP):
        group = range(first, first + GROUP)
        reverses = []
        for h in group:
            total = jnp.zeros((width, width), jnp.float32)
            for level in range(1, bits + 1):
                total = total + jnp.where(is_upper(level), 0, received(level, h)).astype(jnp.float32)
            reverses.append(total.astype(LOW))
        low = spread(reverses)
        near_k = jnp.concatenate([nk_ref[h] for h in group], 1)
        near_v = jnp.concatenate([nv_ref[h] for h in group], 1)
        value = v_ref[:, first * width : (first + GROUP) * width]
        key = k_ref[:, first * width : (first + GROUP) * width]
        gk_buf[first // GROUP] = (near_k + nt(value, low)).astype(LOW)
        gv_buf[first // GROUP] = (near_v + nn(key, low)).astype(LOW)
        send(0, first, gk_buf, gk_hbm)
        send(1, first, gv_buf, gv_hbm)
    pltpu.make_async_copy(gq_buf, gq_hbm, gq_sem).wait()
    for copy in copies:
        copy.wait()


ANY = pl.BlockSpec(memory_space=pl.ANY)
IN_VMEM = pl.BlockSpec(memory_space=pltpu.VMEM)
LIMIT = 16 * 1024 * 1024


def in_hbm(array):
    return pltpu.with_memory_space_constraint(array, pltpu.HBM)


def call(kernel, name, flops, out_shape, operands):
    outs = [pltpu.VMEM(shape, dtype) for shape, dtype in out_shape]
    return pl.pallas_call(
        kernel,
        out_shape=outs,
        in_specs=[IN_VMEM] * len(operands),
        out_specs=[IN_VMEM] * len(outs),
        compiler_params=pltpu.CompilerParams(vmem_limit_bytes=LIMIT),
        cost_estimate=pl.CostEstimate(flops=flops, bytes_accessed=0, transcendentals=0),
        name=name,
    )(*[in_vmem(x) for x in operands])


def on_device(queries, keys, values, out_grad, level_weights):
    tokens = queries.shape[0]
    heads, levels, _ = level_weights.shape
    width = queries.shape[1] // heads
    half = heads // 2
    bits = lax.axis_size(AXES).bit_length() - 1
    scales = level_scales(width, tokens, levels)
    f32 = jnp.float32
    cost = 1000 * tokens * tokens * width
    turned = ((heads, width, tokens), LOW)
    full = ((heads, width, width), LOW)
    halves = (((bits - 2) * half, width, width), LOW)
    weight_rows = ((heads, levels, tokens), f32)
    outs = [turned, halves, halves]
    chosen = pltpu.VMEM((bits - 2, tokens, heads * width), LOW)
    t_v, own, other = pl.pallas_call(
        functools.partial(top_kernel, bits, scales),
        out_shape=[pltpu.VMEM(shape, dtype) for shape, dtype in outs],
        in_specs=[ANY] * 5,
        out_specs=[IN_VMEM] * len(outs),
        scratch_shapes=[
            chosen, chosen, pltpu.VMEM((bits - 2, heads, 1, tokens), f32),
            pltpu.SemaphoreType.DMA((3, bits - 2)),
        ],
        compiler_params=pltpu.CompilerParams(vmem_limit_bytes=LIMIT),
        cost_estimate=pl.CostEstimate(flops=cost, bytes_accessed=0, transcendentals=0),
        name="top_states",
    )(*[in_hbm(x) for x in (queries, keys, values, out_grad, level_weights)])

    def as_f(array):
        return array.astype(f32)

    got_z = flip(own, 2)
    got_d = flip(other, 3)
    (other_x,) = call(copy_kernel, "x_part", cost, [halves], [other])
    got_x = flip(other_x, 1)
    (quad,) = call(sum_kernel, "quad_sum", cost, [halves], [own, got_x, got_z, got_d])
    qt, kt, d1, d2 = call(
        functools.partial(low_kernel, bits, scales), "low_states", cost,
        [turned, turned, full, full], [queries, keys, values, out_grad, level_weights, t_v],
    )
    got_2 = flip(d2, 2)
    (d1,) = call(copy_kernel, "first_level", cost, [full], [d1])
    got_1 = flip(d1, 1)
    sums = []
    for bit in range(2, bits):
        sums.append(quad[:half])
        quad = quad[half:]
        if bit < bits - 1:
            quad = (as_f(quad) + as_f(flip(quad, 1 << bit))).astype(LOW)
    early_half = [swap_halves(x, i + 2, True) for i, x in enumerate(sums)]
    late_half = [swap_halves(x, i + 2, False) for i, x in enumerate(sums)]
    diagonal_2 = flip(got_2, 1)
    flat = ((tokens, heads * width), LOW)
    total, weights, near_k, near_v, early_q = call(
        functools.partial(near_kernel, scales[0]), "near", cost,
        [((heads, width, tokens), f32), weight_rows, *[((heads, tokens, width), f32)] * 2, flat],
        [queries, keys, values, out_grad, level_weights, kt],
    )
    operands = [keys, values, out_grad, level_weights, qt, total, weights, near_k, near_v]
    operands += [early_q, got_1, got_2, diagonal_2, *late_half, *early_half]
    out = jax.ShapeDtypeStruct((tokens, heads * width), LOW)
    return pl.pallas_call(
        functools.partial(far_kernel, bits, scales),
        out_shape=(
            out, out, out, jax.ShapeDtypeStruct((heads, levels, tokens), f32),
            pltpu.VMEM((heads, width, tokens), f32),
        ),
        in_specs=[IN_VMEM] * len(operands),
        out_specs=(ANY,) * 4 + (IN_VMEM,),
        input_output_aliases={5: 4},
        scratch_shapes=[pltpu.VMEM(*flat)]
        + [pltpu.VMEM((heads // GROUP, tokens, GROUP * width), LOW)] * 2
        + [
            pltpu.VMEM((heads, levels, tokens), f32),
            pltpu.SemaphoreType.DMA((2, heads)),
            pltpu.SemaphoreType.DMA,
            pltpu.SemaphoreType.DMA,
        ],
        compiler_params=pltpu.CompilerParams(vmem_limit_bytes=LIMIT),
        cost_estimate=pl.CostEstimate(flops=cost, bytes_accessed=0, transcendentals=0),
        name="far",
    )(*[in_vmem(x) for x in operands])[:4]


def solution(mesh):
    rows = P(("groups", "seq", "heads"), "sub")
    weights = P("sub", None, ("groups", "seq", "heads"))
    return jax.shard_map(
        on_device,
        mesh=mesh,
        in_specs=(rows, rows, rows, rows, weights),
        out_specs=(rows, rows, rows, weights),
        check_vma=False,
    )
```

```python
import functools
import math

import jax
import jax.numpy as jnp
from jax import lax
from jax.experimental import pallas as pl
from jax.experimental.pallas import tpu as pltpu
from jax.sharding import PartitionSpec as P

AXES = ("seq", "heads")
LOW = jnp.bfloat16
ROWS = 256
GROUP = 2


def nt(left, right):
    return lax.dot_general(
        left, right, (((1,), (1,)), ((), ())), preferred_element_type=jnp.float32
    )


def nn(left, right):
    return jnp.dot(left, right, preferred_element_type=jnp.float32)


def flip(block, mask):
    size = lax.axis_size(AXES)
    return lax.ppermute(block, AXES, [(i, i ^ mask) for i in range(size)])


def swap_halves(block, bit, upper_turns):
    routes = []
    for i in range(lax.axis_size(AXES)):
        upper = (i >> bit) & 1 == 1
        routes.append((i, i ^ (1 << bit) ^ (1 if upper == upper_turns else 0)))
    return lax.ppermute(block, AXES, routes)


def block_index():
    return lax.axis_index("seq") * lax.axis_size("heads") + lax.axis_index("heads")


def head(ref, h, width, rows=slice(None)):
    return ref[rows, h * width : (h + 1) * width]


def in_vmem(array):
    return pltpu.with_memory_space_constraint(array, pltpu.VMEM)


def level_scales(width, tokens, count):
    base = 1.0 / math.sqrt(width * tokens)
    return [base] + [base / math.sqrt(2.0 ** (level - 1)) for level in range(1, count)]


def top_kernel(
    bits, scales, q_hbm, k_hbm, v_hbm, g_hbm, w_hbm, t_out, own_out, other_out, left_buf, right_buf, w_buf, sems
):
    heads, width, tokens = t_out.shape
    half = heads // 2
    place = block_index()
    low_bit = place & 1

    def states(index, upper):
        level = index + 3
        left, right = (q_hbm, g_hbm) if upper else (k_hbm, v_hbm)
        copies = [
            pltpu.make_async_copy(left, left_buf.at[index], sems.at[0, index]),
            pltpu.make_async_copy(right, right_buf.at[index], sems.at[1, index]),
        ]
        if upper:
            level_row = w_hbm.at[:, pl.ds(level, 1), :]
            copies.append(pltpu.make_async_copy(level_row, w_buf.at[index], sems.at[2, index]))
        for copy in copies:
            copy.start()
        for copy in copies:
            copy.wait()
        held = []
        for first in range(0, heads, GROUP):
            lefts = []
            for h in range(first, first + GROUP):
                turned = head(left_buf.at[index], h, width).T
                if level == bits:
                    t_out[h] = turned
                if upper:
                    turned = (w_buf[index, h] * turned.astype(jnp.float32)).astype(LOW)
                lefts.append(turned)
            columns = slice(first * width, (first + GROUP) * width)
            product = nn(jnp.concatenate(lefts, 0), right_buf[index, :, columns])
            for i in range(GROUP):
                block = slice(i * width, i * width + width)
                state = product[block, block]
                held.append((scales[level] * state if upper else state).astype(LOW))
        for i in range(half):
            low, high = held[i], held[half + i]
            own_out[index * half + i] = jnp.where(low_bit == 0, low, high)
            other_out[index * half + i] = jnp.where(low_bit == 0, high, low)

    for index in range(bits - 2):
        bit = (place >> (index + 2)) & 1
        for value in (0, 1):

            @pl.when(bit == value)
            def _():
                states(index, value == 1)


def mixed_state(level, scale, h, place, query_t, key_t, w_ref, v_ref, g_ref):
    width = query_t.shape[0]
    upper = ((place >> (level - 1)) & 1) == 1
    scaled = (w_ref[h, pl.ds(level, 1), :] * query_t.astype(jnp.float32)).astype(LOW)
    left = jnp.where(upper, scaled, key_t)
    right = jnp.where(upper, head(g_ref, h, width), head(v_ref, h, width))
    return (jnp.where(upper, scale, 1.0) * nn(left, right)).astype(LOW)


def low_kernel(bits, scales, q_ref, k_ref, v_ref, g_ref, w_ref, t_ref, qt_out, kt_out, d1_out, d2_out):
    heads, width = t_ref.shape[:2]
    place = block_index()
    top = ((place >> (bits - 1)) & 1) == 1
    for h in range(heads):
        turned = t_ref[h]
        other = jnp.where(top, head(k_ref, h, width), head(q_ref, h, width)).T
        query_t = jnp.where(top, turned, other)
        key_t = jnp.where(top, other, turned)
        qt_out[h] = query_t
        kt_out[h] = key_t
        for level, out in ((1, d1_out), (2, d2_out)):
            out[h] = mixed_state(
                level, scales[level], h, place, query_t, key_t, w_ref, v_ref, g_ref
            )


def near_head(scale, h, q_ref, k_ref, v_ref, g_ref, w_ref, kt_ref, nk_out, nv_out):
    width, tokens = kt_ref.shape[1:]
    rows = min(ROWS, tokens)
    factor = scale * w_ref[h, pl.ds(0, 1), :]
    back, weight = [], []
    for start in range(0, tokens, rows):
        left = tokens - start
        key = head(k_ref, h, width, slice(start, start + rows))
        value = head(v_ref, h, width, slice(start, start + rows))
        query = head(q_ref, h, width, slice(start, None))
        grad = head(g_ref, h, width, slice(start, None))
        scores = nt(key, query)
        dots = nt(value, grad)
        allowed = lax.broadcasted_iota(jnp.int32, (rows, left), 0) <= lax.broadcasted_iota(
            jnp.int32, (rows, left), 1
        )
        scores = jnp.where(allowed, scores, 0.0)
        dots = jnp.where(allowed, dots, 0.0)
        part = jnp.sum(scores * dots, axis=0, keepdims=True)
        now = factor[:, start:]
        grad_mix = (now * dots).astype(LOW)
        score_mix = (now * scores).astype(LOW)
        nk_out[h, start : start + rows, :] = nn(grad_mix, query)
        nv_out[h, start : start + rows, :] = nn(score_mix, grad)
        back.append(nn(kt_ref[h, :, start : start + rows], grad_mix))
        weight.append(scale * part)
    return back, weight


def store_sums(ref, h, rows, parts):
    tokens = parts[0].shape[1]
    for i, part in enumerate(parts):
        start = tokens - part.shape[1]
        if i == 0:
            ref[h, rows, :] = part
        else:
            ref[h, rows, start:] += part


def near_kernel(scale, *refs):
    ins, (sum_out, gw_out, nk_out, nv_out, gq_out) = refs[:6], refs[6:]
    for h in range(sum_out.shape[0]):
        gw_out[h] = jnp.zeros(gw_out.shape[1:], jnp.float32)
        back, weight = near_head(scale, h, *ins, nk_out, nv_out)
        store_sums(sum_out, h, slice(None), back)
        store_sums(gw_out, h, pl.ds(0, 1), weight)

    @pl.when(block_index() == 0)
    def _():
        store_queries(sum_out, gq_out)


def store_queries(sum_ref, gq_ref):
    heads, width, _ = sum_ref.shape
    for h in range(heads):
        gq_ref[:, h * width : (h + 1) * width] = sum_ref[h].astype(LOW).T


def copy_kernel(source, out):
    out[...] = source[...]


def sum_kernel(*refs):
    *parts, out = refs
    total = parts[0][...].astype(jnp.float32)
    for part in parts[1:]:
        total = total + part[...].astype(jnp.float32)
    out[...] = total.astype(LOW)


def spread(blocks):
    zeros = jnp.zeros_like(blocks[0])
    return jnp.concatenate(
        [
            jnp.concatenate([block if i == j else zeros for j in range(len(blocks))], 1)
            for i, block in enumerate(blocks)
        ],
        0,
    )


def far_kernel(bits, scales, *refs):
    k_ref, v_ref, g_ref, w_ref, qt_ref, _, weight_ref, nk_ref, nv_ref = refs[:9]
    (gq_ref, r1_ref, z2_ref, d2_ref), refs = refs[9:13], refs[13:]
    late_refs, early_refs, refs = refs[: bits - 2], refs[bits - 2 : 2 * bits - 4], refs[2 * bits - 4 :]
    gq_hbm, gk_hbm, gv_hbm, gw_hbm, sum_ref, gq_buf, gk_buf, gv_buf, gw_buf, sems, w_sem, gq_sem = refs
    heads, width, tokens = sum_ref.shape
    half = heads // 2
    place = block_index()
    low_bit = place & 1
    copies = []

    def is_upper(level):
        return ((place >> (level - 1)) & 1) == 1

    def received(level, h):
        if level == 1:
            return r1_ref[h]
        if level == 2:
            return z2_ref[h].astype(jnp.float32) + d2_ref[h].astype(jnp.float32)
        early_ref, late_ref = early_refs[level - 3], late_refs[level - 3]
        early = (low_bit == h // half) == is_upper(level)
        return jnp.where(early, early_ref[h % half], late_ref[h % half])

    def send(i, first, buf, hbm):
        span = pl.ds(first * width, GROUP * width)
        copy = pltpu.make_async_copy(buf.at[first // GROUP], hbm.at[:, span], sems.at[i, first])
        copy.start()
        copies.append(copy)

    @pl.when(place == 0)
    def _():
        pltpu.make_async_copy(gq_ref, gq_hbm, gq_sem).start()

    gw_buf[...] = weight_ref[...]
    for level in range(1, bits + 1):

        @pl.when(is_upper(level))
        def _():
            for first in range(0, heads, GROUP):
                group = range(first, first + GROUP)
                siblings = spread([received(level, h).astype(LOW) for h in group])
                products = nt(siblings, g_ref[:, first * width : (first + GROUP) * width])
                for i, h in enumerate(group):
                    mine = products[i * width : i * width + width]
                    sum_ref[h] += (scales[level] * w_ref[h, pl.ds(level, 1), :]) * mine
                    gw_buf[h, pl.ds(level, 1), :] = scales[level] * jnp.sum(
                        mine * qt_ref[h].astype(jnp.float32), axis=0, keepdims=True
                    )

    copy = pltpu.make_async_copy(gw_buf, gw_hbm, w_sem)
    copy.start()
    copies.append(copy)

    @pl.when(place != 0)
    def _():
        store_queries(sum_ref, gq_buf)
        pltpu.make_async_copy(gq_buf, gq_hbm, gq_sem).start()

    for first in range(0, heads, GROUP):
        group = range(first, first + GROUP)
        reverses = []
        for h in group:
            total = jnp.zeros((width, width), jnp.float32)
            for level in range(1, bits + 1):
                total = total + jnp.where(is_upper(level), 0, received(level, h)).astype(jnp.float32)
            reverses.append(total.astype(LOW))
        low = spread(reverses)
        near_k = jnp.concatenate([nk_ref[h] for h in group], 1)
        near_v = jnp.concatenate([nv_ref[h] for h in group], 1)
        value = v_ref[:, first * width : (first + GROUP) * width]
        key = k_ref[:, first * width : (first + GROUP) * width]
        gk_buf[first // GROUP] = (near_k + nt(value, low)).astype(LOW)
        send(0, first, gk_buf, gk_hbm)
        gv_buf[first // GROUP] = (near_v + nn(key, low)).astype(LOW)
        send(1, first, gv_buf, gv_hbm)
    pltpu.make_async_copy(gq_buf, gq_hbm, gq_sem).wait()
    for copy in copies:
        copy.wait()


ANY = pl.BlockSpec(memory_space=pl.ANY)
IN_VMEM = pl.BlockSpec(memory_space=pltpu.VMEM)
LIMIT = 16 * 1024 * 1024


def in_hbm(array):
    return pltpu.with_memory_space_constraint(array, pltpu.HBM)


def call(kernel, name, flops, out_shape, operands):
    outs = [pltpu.VMEM(shape, dtype) for shape, dtype in out_shape]
    return pl.pallas_call(
        kernel,
        out_shape=outs,
        in_specs=[IN_VMEM] * len(operands),
        out_specs=[IN_VMEM] * len(outs),
        compiler_params=pltpu.CompilerParams(vmem_limit_bytes=LIMIT),
        cost_estimate=pl.CostEstimate(flops=flops, bytes_accessed=0, transcendentals=0),
        name=name,
    )(*[in_vmem(x) for x in operands])


def on_device(queries, keys, values, out_grad, level_weights):
    tokens = queries.shape[0]
    heads, levels, _ = level_weights.shape
    width = queries.shape[1] // heads
    half = heads // 2
    bits = lax.axis_size(AXES).bit_length() - 1
    scales = level_scales(width, tokens, levels)
    f32 = jnp.float32
    cost = 1000 * tokens * tokens * width
    turned = ((heads, width, tokens), LOW)
    full = ((heads, width, width), LOW)
    halves = (((bits - 2) * half, width, width), LOW)
    weight_rows = ((heads, levels, tokens), f32)
    outs = [turned, halves, halves]
    chosen = pltpu.VMEM((bits - 2, tokens, heads * width), LOW)
    t_v, own, other = pl.pallas_call(
        functools.partial(top_kernel, bits, scales),
        out_shape=[pltpu.VMEM(shape, dtype) for shape, dtype in outs],
        in_specs=[ANY] * 5,
        out_specs=[IN_VMEM] * len(outs),
        scratch_shapes=[
            chosen, chosen, pltpu.VMEM((bits - 2, heads, 1, tokens), f32),
            pltpu.SemaphoreType.DMA((3, bits - 2)),
        ],
        compiler_params=pltpu.CompilerParams(vmem_limit_bytes=LIMIT),
        cost_estimate=pl.CostEstimate(flops=cost, bytes_accessed=0, transcendentals=0),
        name="top_states",
    )(*[in_hbm(x) for x in (queries, keys, values, out_grad, level_weights)])

    def as_f(array):
        return array.astype(f32)

    got_z = flip(own, 2)
    got_d = flip(other, 3)
    (other_x,) = call(copy_kernel, "x_part", cost, [halves], [other])
    got_x = flip(other_x, 1)
    (quad,) = call(sum_kernel, "quad_sum", cost, [halves], [own, got_x, got_z, got_d])
    qt, kt, d1, d2 = call(
        functools.partial(low_kernel, bits, scales), "low_states", cost,
        [turned, turned, full, full], [queries, keys, values, out_grad, level_weights, t_v],
    )
    got_2 = flip(d2, 2)
    (d1,) = call(copy_kernel, "first_level", cost, [full], [d1])
    got_1 = flip(d1, 1)
    sums = []
    for bit in range(2, bits):
        sums.append(quad[:half])
        quad = quad[half:]
        if bit < bits - 1:
            quad = (as_f(quad) + as_f(flip(quad, 1 << bit))).astype(LOW)
    early_half = [swap_halves(x, i + 2, True) for i, x in enumerate(sums)]
    late_half = [swap_halves(x, i + 2, False) for i, x in enumerate(sums)]
    diagonal_2 = flip(got_2, 1)
    flat = ((tokens, heads * width), LOW)
    total, weights, near_k, near_v, early_q = call(
        functools.partial(near_kernel, scales[0]), "near", cost,
        [((heads, width, tokens), f32), weight_rows, *[((heads, tokens, width), f32)] * 2, flat],
        [queries, keys, values, out_grad, level_weights, kt],
    )
    operands = [keys, values, out_grad, level_weights, qt, total, weights, near_k, near_v]
    operands += [early_q, got_1, got_2, diagonal_2, *late_half, *early_half]
    out = jax.ShapeDtypeStruct((tokens, heads * width), LOW)
    return pl.pallas_call(
        functools.partial(far_kernel, bits, scales),
        out_shape=(
            out, out, out, jax.ShapeDtypeStruct((heads, levels, tokens), f32),
            pltpu.VMEM((heads, width, tokens), f32),
        ),
        in_specs=[IN_VMEM] * len(operands),
        out_specs=(ANY,) * 4 + (IN_VMEM,),
        input_output_aliases={5: 4},
        scratch_shapes=[pltpu.VMEM(*flat)]
        + [pltpu.VMEM((heads // GROUP, tokens, GROUP * width), LOW)] * 2
        + [
            pltpu.VMEM((heads, levels, tokens), f32),
            pltpu.SemaphoreType.DMA((2, heads)),
            pltpu.SemaphoreType.DMA,
            pltpu.SemaphoreType.DMA,
        ],
        compiler_params=pltpu.CompilerParams(vmem_limit_bytes=LIMIT),
        cost_estimate=pl.CostEstimate(flops=cost, bytes_accessed=0, transcendentals=0),
        name="far",
    )(*[in_vmem(x) for x in operands])[:4]


def solution(mesh):
    rows = P(("groups", "seq", "heads"), "sub")
    weights = P("sub", None, ("groups", "seq", "heads"))
    return jax.shard_map(
        on_device,
        mesh=mesh,
        in_specs=(rows, rows, rows, rows, weights),
        out_specs=(rows, rows, rows, weights),
        check_vma=False,
    )
```

```python
import functools
import math

import jax
import jax.numpy as jnp
from jax import lax
from jax.experimental import pallas as pl
from jax.experimental.pallas import tpu as pltpu
from jax.sharding import PartitionSpec as P

AXES = ("seq", "heads")
LOW = jnp.bfloat16
ROWS = 256
GROUP = 2


def nt(left, right):
    return lax.dot_general(
        left, right, (((1,), (1,)), ((), ())), preferred_element_type=jnp.float32
    )


def nn(left, right):
    return jnp.dot(left, right, preferred_element_type=jnp.float32)


def flip(block, mask):
    size = lax.axis_size(AXES)
    return lax.ppermute(block, AXES, [(i, i ^ mask) for i in range(size)])


def swap_halves(block, bit, upper_turns):
    routes = []
    for i in range(lax.axis_size(AXES)):
        upper = (i >> bit) & 1 == 1
        routes.append((i, i ^ (1 << bit) ^ (1 if upper == upper_turns else 0)))
    return lax.ppermute(block, AXES, routes)


def block_index():
    return lax.axis_index("seq") * lax.axis_size("heads") + lax.axis_index("heads")


def head(ref, h, width, rows=slice(None)):
    return ref[rows, h * width : (h + 1) * width]


def in_vmem(array):
    return pltpu.with_memory_space_constraint(array, pltpu.VMEM)


def level_scales(width, tokens, count):
    base = 1.0 / math.sqrt(width * tokens)
    return [base] + [base / math.sqrt(2.0 ** (level - 1)) for level in range(1, count)]


def top_kernel(
    bits, scales, q_hbm, k_hbm, v_hbm, g_hbm, w_hbm, t_out, own_out, other_out, left_buf, right_buf, w_buf, sems
):
    heads, width, tokens = t_out.shape
    half = heads // 2
    place = block_index()
    low_bit = place & 1

    def states(index, upper):
        level = index + 3
        left, right = (q_hbm, g_hbm) if upper else (k_hbm, v_hbm)
        copies = [
            pltpu.make_async_copy(left, left_buf.at[index], sems.at[0, index]),
            pltpu.make_async_copy(right, right_buf.at[index], sems.at[1, index]),
        ]
        if upper:
            level_row = w_hbm.at[:, pl.ds(level, 1), :]
            copies.append(pltpu.make_async_copy(level_row, w_buf.at[index], sems.at[2, index]))
        for copy in copies:
            copy.start()
        copies[0].wait()
        if upper:
            copies[2].wait()
        held = []
        for first in range(0, heads, GROUP):
            lefts = []
            for h in range(first, first + GROUP):
                turned = head(left_buf.at[index], h, width).T
                if level == bits:
                    t_out[h] = turned
                if upper:
                    turned = (w_buf[index, h] * turned.astype(jnp.float32)).astype(LOW)
                lefts.append(turned)
            if first == 0:
                copies[1].wait()
            columns = slice(first * width, (first + GROUP) * width)
            product = nn(jnp.concatenate(lefts, 0), right_buf[index, :, columns])
            for i in range(GROUP):
                block = slice(i * width, i * width + width)
                state = product[block, block]
                held.append((scales[level] * state if upper else state).astype(LOW))
        for i in range(half):
            low, high = held[i], held[half + i]
            own_out[index * half + i] = jnp.where(low_bit == 0, low, high)
            other_out[index * half + i] = jnp.where(low_bit == 0, high, low)

    for index in range(bits - 2):
        bit = (place >> (index + 2)) & 1
        for value in (0, 1):

            @pl.when(bit == value)
            def _():
                states(index, value == 1)


def mixed_state(level, scale, h, place, query_t, key_t, w_ref, v_ref, g_ref):
    width = query_t.shape[0]
    upper = ((place >> (level - 1)) & 1) == 1
    scaled = (w_ref[h, pl.ds(level, 1), :] * query_t.astype(jnp.float32)).astype(LOW)
    left = jnp.where(upper, scaled, key_t)
    right = jnp.where(upper, head(g_ref, h, width), head(v_ref, h, width))
    return (jnp.where(upper, scale, 1.0) * nn(left, right)).astype(LOW)


def low_kernel(bits, scales, q_ref, k_ref, v_ref, g_ref, w_ref, t_ref, qt_out, kt_out, d1_out, d2_out):
    heads, width = t_ref.shape[:2]
    place = block_index()
    top = ((place >> (bits - 1)) & 1) == 1
    for h in range(heads):
        turned = t_ref[h]
        other = jnp.where(top, head(k_ref, h, width), head(q_ref, h, width)).T
        query_t = jnp.where(top, turned, other)
        key_t = jnp.where(top, other, turned)
        qt_out[h] = query_t
        kt_out[h] = key_t
        for level, out in ((1, d1_out), (2, d2_out)):
            out[h] = mixed_state(
                level, scales[level], h, place, query_t, key_t, w_ref, v_ref, g_ref
            )


def near_head(scale, h, q_ref, k_ref, v_ref, g_ref, w_ref, kt_ref, nk_out, nv_out):
    width, tokens = kt_ref.shape[1:]
    rows = min(ROWS, tokens)
    factor = scale * w_ref[h, pl.ds(0, 1), :]
    back, weight = [], []
    for start in range(0, tokens, rows):
        left = tokens - start
        key = head(k_ref, h, width, slice(start, start + rows))
        value = head(v_ref, h, width, slice(start, start + rows))
        query = head(q_ref, h, width, slice(start, None))
        grad = head(g_ref, h, width, slice(start, None))
        scores = nt(key, query)
        dots = nt(value, grad)
        allowed = lax.broadcasted_iota(jnp.int32, (rows, left), 0) <= lax.broadcasted_iota(
            jnp.int32, (rows, left), 1
        )
        scores = jnp.where(allowed, scores, 0.0)
        dots = jnp.where(allowed, dots, 0.0)
        part = jnp.sum(scores * dots, axis=0, keepdims=True)
        now = factor[:, start:]
        grad_mix = (now * dots).astype(LOW)
        score_mix = (now * scores).astype(LOW)
        nk_out[h, start : start + rows, :] = nn(grad_mix, query)
        nv_out[h, start : start + rows, :] = nn(score_mix, grad)
        back.append(nn(kt_ref[h, :, start : start + rows], grad_mix))
        weight.append(scale * part)
    return back, weight


def store_sums(ref, h, rows, parts):
    tokens = parts[0].shape[1]
    for i, part in enumerate(parts):
        start = tokens - part.shape[1]
        if i == 0:
            ref[h, rows, :] = part
        else:
            ref[h, rows, start:] += part


def near_kernel(scale, *refs):
    ins, (sum_out, gw_out, nk_out, nv_out, gq_out) = refs[:6], refs[6:]
    for h in range(sum_out.shape[0]):
        gw_out[h] = jnp.zeros(gw_out.shape[1:], jnp.float32)
        back, weight = near_head(scale, h, *ins, nk_out, nv_out)
        store_sums(sum_out, h, slice(None), back)
        store_sums(gw_out, h, pl.ds(0, 1), weight)

    @pl.when(block_index() == 0)
    def _():
        store_queries(sum_out, gq_out)


def store_queries(sum_ref, gq_ref):
    heads, width, _ = sum_ref.shape
    for h in range(heads):
        gq_ref[:, h * width : (h + 1) * width] = sum_ref[h].astype(LOW).T


def copy_kernel(source, out):
    out[...] = source[...]


def sum_kernel(*refs):
    *parts, out = refs
    total = parts[0][...].astype(jnp.float32)
    for part in parts[1:]:
        total = total + part[...].astype(jnp.float32)
    out[...] = total.astype(LOW)


def spread(blocks):
    zeros = jnp.zeros_like(blocks[0])
    return jnp.concatenate(
        [
            jnp.concatenate([block if i == j else zeros for j in range(len(blocks))], 1)
            for i, block in enumerate(blocks)
        ],
        0,
    )


def far_kernel(bits, scales, *refs):
    k_ref, v_ref, g_ref, w_ref, qt_ref, _, weight_ref, nk_ref, nv_ref = refs[:9]
    (gq_ref, r1_ref, z2_ref, d2_ref), refs = refs[9:13], refs[13:]
    late_refs, early_refs, refs = refs[: bits - 2], refs[bits - 2 : 2 * bits - 4], refs[2 * bits - 4 :]
    gq_hbm, gk_hbm, gv_hbm, gw_hbm, sum_ref, gq_buf, gk_buf, gv_buf, gw_buf, sems, w_sem, gq_sem = refs
    heads, width, tokens = sum_ref.shape
    half = heads // 2
    place = block_index()
    low_bit = place & 1
    copies = []

    def is_upper(level):
        return ((place >> (level - 1)) & 1) == 1

    def received(level, h):
        if level == 1:
            return r1_ref[h]
        if level == 2:
            return z2_ref[h].astype(jnp.float32) + d2_ref[h].astype(jnp.float32)
        early_ref, late_ref = early_refs[level - 3], late_refs[level - 3]
        early = (low_bit == h // half) == is_upper(level)
        return jnp.where(early, early_ref[h % half], late_ref[h % half])

    def send(i, first, buf, hbm):
        span = pl.ds(first * width, GROUP * width)
        copy = pltpu.make_async_copy(buf.at[first // GROUP], hbm.at[:, span], sems.at[i, first])
        copy.start()
        copies.append(copy)

    @pl.when(place == 0)
    def _():
        pltpu.make_async_copy(gq_ref, gq_hbm, gq_sem).start()

    gw_buf[...] = weight_ref[...]
    for level in range(1, bits + 1):

        @pl.when(is_upper(level))
        def _():
            for first in range(0, heads, GROUP):
                group = range(first, first + GROUP)
                siblings = spread([received(level, h).astype(LOW) for h in group])
                products = nt(siblings, g_ref[:, first * width : (first + GROUP) * width])
                for i, h in enumerate(group):
                    mine = products[i * width : i * width + width]
                    sum_ref[h] += (scales[level] * w_ref[h, pl.ds(level, 1), :]) * mine
                    gw_buf[h, pl.ds(level, 1), :] = scales[level] * jnp.sum(
                        mine * qt_ref[h].astype(jnp.float32), axis=0, keepdims=True
                    )

    copy = pltpu.make_async_copy(gw_buf, gw_hbm, w_sem)
    copy.start()
    copies.append(copy)

    @pl.when(place != 0)
    def _():
        store_queries(sum_ref, gq_buf)
        pltpu.make_async_copy(gq_buf, gq_hbm, gq_sem).start()

    for first in range(0, heads, GROUP):
        group = range(first, first + GROUP)
        reverses = []
        for h in group:
            total = jnp.zeros((width, width), jnp.float32)
            for level in range(1, bits + 1):
                total = total + jnp.where(is_upper(level), 0, received(level, h)).astype(jnp.float32)
            reverses.append(total.astype(LOW))
        low = spread(reverses)
        near_k = jnp.concatenate([nk_ref[h] for h in group], 1)
        near_v = jnp.concatenate([nv_ref[h] for h in group], 1)
        value = v_ref[:, first * width : (first + GROUP) * width]
        key = k_ref[:, first * width : (first + GROUP) * width]
        gk_buf[first // GROUP] = (near_k + nt(value, low)).astype(LOW)
        send(0, first, gk_buf, gk_hbm)
        gv_buf[first // GROUP] = (near_v + nn(key, low)).astype(LOW)
        send(1, first, gv_buf, gv_hbm)
    pltpu.make_async_copy(gq_buf, gq_hbm, gq_sem).wait()
    for copy in copies:
        copy.wait()


ANY = pl.BlockSpec(memory_space=pl.ANY)
IN_VMEM = pl.BlockSpec(memory_space=pltpu.VMEM)
LIMIT = 16 * 1024 * 1024


def in_hbm(array):
    return pltpu.with_memory_space_constraint(array, pltpu.HBM)


def call(kernel, name, flops, out_shape, operands):
    outs = [pltpu.VMEM(shape, dtype) for shape, dtype in out_shape]
    return pl.pallas_call(
        kernel,
        out_shape=outs,
        in_specs=[IN_VMEM] * len(operands),
        out_specs=[IN_VMEM] * len(outs),
        compiler_params=pltpu.CompilerParams(vmem_limit_bytes=LIMIT),
        cost_estimate=pl.CostEstimate(flops=flops, bytes_accessed=0, transcendentals=0),
        name=name,
    )(*[in_vmem(x) for x in operands])


def on_device(queries, keys, values, out_grad, level_weights):
    tokens = queries.shape[0]
    heads, levels, _ = level_weights.shape
    width = queries.shape[1] // heads
    half = heads // 2
    bits = lax.axis_size(AXES).bit_length() - 1
    scales = level_scales(width, tokens, levels)
    f32 = jnp.float32
    cost = 1000 * tokens * tokens * width
    turned = ((heads, width, tokens), LOW)
    full = ((heads, width, width), LOW)
    halves = (((bits - 2) * half, width, width), LOW)
    weight_rows = ((heads, levels, tokens), f32)
    outs = [turned, halves, halves]
    chosen = pltpu.VMEM((bits - 2, tokens, heads * width), LOW)
    t_v, own, other = pl.pallas_call(
        functools.partial(top_kernel, bits, scales),
        out_shape=[pltpu.VMEM(shape, dtype) for shape, dtype in outs],
        in_specs=[ANY] * 5,
        out_specs=[IN_VMEM] * len(outs),
        scratch_shapes=[
            chosen, chosen, pltpu.VMEM((bits - 2, heads, 1, tokens), f32),
            pltpu.SemaphoreType.DMA((3, bits - 2)),
        ],
        compiler_params=pltpu.CompilerParams(vmem_limit_bytes=LIMIT),
        cost_estimate=pl.CostEstimate(flops=cost, bytes_accessed=0, transcendentals=0),
        name="top_states",
    )(*[in_hbm(x) for x in (queries, keys, values, out_grad, level_weights)])

    def as_f(array):
        return array.astype(f32)

    got_z = flip(own, 2)
    got_d = flip(other, 3)
    (other_x,) = call(copy_kernel, "x_part", cost, [halves], [other])
    got_x = flip(other_x, 1)
    (quad,) = call(sum_kernel, "quad_sum", cost, [halves], [own, got_x, got_z, got_d])
    qt, kt, d1, d2 = call(
        functools.partial(low_kernel, bits, scales), "low_states", cost,
        [turned, turned, full, full], [queries, keys, values, out_grad, level_weights, t_v],
    )
    got_2 = flip(d2, 2)
    (d1,) = call(copy_kernel, "first_level", cost, [full], [d1])
    got_1 = flip(d1, 1)
    sums = []
    for bit in range(2, bits):
        sums.append(quad[:half])
        quad = quad[half:]
        if bit < bits - 1:
            quad = (as_f(quad) + as_f(flip(quad, 1 << bit))).astype(LOW)
    early_half = [swap_halves(x, i + 2, True) for i, x in enumerate(sums)]
    late_half = [swap_halves(x, i + 2, False) for i, x in enumerate(sums)]
    diagonal_2 = flip(got_2, 1)
    flat = ((tokens, heads * width), LOW)
    total, weights, near_k, near_v, early_q = call(
        functools.partial(near_kernel, scales[0]), "near", cost,
        [((heads, width, tokens), f32), weight_rows, *[((heads, tokens, width), f32)] * 2, flat],
        [queries, keys, values, out_grad, level_weights, kt],
    )
    operands = [keys, values, out_grad, level_weights, qt, total, weights, near_k, near_v]
    operands += [early_q, got_1, got_2, diagonal_2, *late_half, *early_half]
    out = jax.ShapeDtypeStruct((tokens, heads * width), LOW)
    return pl.pallas_call(
        functools.partial(far_kernel, bits, scales),
        out_shape=(
            out, out, out, jax.ShapeDtypeStruct((heads, levels, tokens), f32),
            pltpu.VMEM((heads, width, tokens), f32),
        ),
        in_specs=[IN_VMEM] * len(operands),
        out_specs=(ANY,) * 4 + (IN_VMEM,),
        input_output_aliases={5: 4},
        scratch_shapes=[pltpu.VMEM(*flat)]
        + [pltpu.VMEM((heads // GROUP, tokens, GROUP * width), LOW)] * 2
        + [
            pltpu.VMEM((heads, levels, tokens), f32),
            pltpu.SemaphoreType.DMA((2, heads)),
            pltpu.SemaphoreType.DMA,
            pltpu.SemaphoreType.DMA,
        ],
        compiler_params=pltpu.CompilerParams(vmem_limit_bytes=LIMIT),
        cost_estimate=pl.CostEstimate(flops=cost, bytes_accessed=0, transcendentals=0),
        name="far",
    )(*[in_vmem(x) for x in operands])[:4]


def solution(mesh):
    rows = P(("groups", "seq", "heads"), "sub")
    weights = P("sub", None, ("groups", "seq", "heads"))
    return jax.shard_map(
        on_device,
        mesh=mesh,
        in_specs=(rows, rows, rows, rows, weights),
        out_specs=(rows, rows, rows, weights),
        check_vma=False,
    )
```
